256 devices in a mesh: section: 2 (over y_lo), row: 16 (over z, y_hi), col: 8 (over x, core).
Axes of the slice: x: 4, y: 4 (y_hi: 2, y_lo: 2; y = y_hi * 2 + y_lo), z: 8, core: 2. Of those that a mesh axis runs over, the one named last changes fastest.
Arguments:
- tokens: float32 [4, 1024, 3072], P(None, 'row', 'col'), may hold values from -30 to 30
- batch_order: int32 [4], replicated, may hold values from 0 to 3, each once
- modulation: float32 [4, 5, 3072], replicated, may hold values from -3 to 3
- expand_weight: bfloat16 [3072, 12288], P('row', 'col'), may hold values from -0.109375 to 0.109375
- expand_bias: float32 [12288], P('col'), may hold values from -3 to 3
- reduce_weight: bfloat16 [12288, 3072], P('col', 'row'), may hold values from -0.0546875 to 0.0546875
- reduce_bias: float32 [3072], P('col'), may hold values from -3 to 3
- patch_weight: float32 [3072, 64], P('col'), may hold values from -0.109375 to 0.109375
- patch_bias: float32 [64], replicated, may hold values from -3 to 3
- latent_kernel: float32 [3, 3, 16, 512], replicated, may hold values from -0.5 to 0.5
- latent_bias: float32 [512], replicated, may hold values from -4 to 4
- group_gain: float32 [512], replicated, may hold values from 0.1 to 1.9
- group_shift: float32 [512], replicated, may hold values from -3 to 3
- decode_kernel: bfloat16 [3, 3, 512, 512], P(None, None, None, 'section'), may hold values from -0.09375 to 0.09375
- decode_bias: float32 [512], P('section'), may hold values from -3 to 3
Outputs:
- decoded: float32 [4, 128, 128, 512], P(None, 'row', 'col', 'section')
The draws below stay inside these ranges and needn't reach their ends.
Inputs may be any that keep to these rules, and one draw needn't show every extreme that they name: `batch_order`: a permutation of the 4 micro-batches.
All inputs are finite; a program needn't handle non-finite values.
Results may differ from the reference program's by a relative error of at most 0.0025.
Values may be sent and summed in bfloat16 or wider, within the bound.
A program may use at most 128 MiB of HBM per device.

```python
import jax
import jax.numpy as jnp
from jax import lax

D = 3072
FF = 12288
LC = 16
VC = 512
GROUPS = 32
MB = 4
PR = 2
PCOLS = 4
PC = 64
TOKENS = 1024
N_ROW = 16
N_COL = 8


def draw_tokens(key, part):
    key = jax.random.fold_in(key, 7)
    noise_key = jax.random.fold_in(key, 0)
    direction_key = jax.random.fold_in(key, 1)
    tilt_key = jax.random.fold_in(key, 3)
    sign_key = jax.random.fold_in(key, 4)
    position = jnp.arange(TOKENS, dtype=jnp.float32)[None, :, None] / (TOKENS - 1)
    feature = 2.0 * jnp.arange(D, dtype=jnp.float32)[None, None, :] / (D - 1) - 1.0
    direction = jnp.clip(jax.random.normal(direction_key, (MB, 1, D), jnp.float32), -4.0, 4.0)
    tilt_size = jax.random.uniform(tilt_key, (MB, 1, 1), jnp.float32, 2.0, 3.0)
    tilt_sign = jnp.where(jax.random.uniform(sign_key, (MB, 1, 1), jnp.float32) < 0.5, -1.0, 1.0)
    tilt = tilt_size * tilt_sign * feature
    jitter = jnp.clip(jax.random.normal(noise_key, (MB, TOKENS, D), jnp.float32), -4.0, 4.0)
    spread = jitter + tilt
    return spread + 2.0 * position * direction


def shard_levels(stream_key, dims, cuts, smallest, high):
    level, own = 1.0, jax.random.fold_in(stream_key, 6)
    for dim, parts in cuts:
        draws = jnp.exp(jax.random.uniform(jax.random.fold_in(own, dim), (parts,), jnp.float32, smallest / len(cuts), high / len(cuts)))
        level = level * jnp.repeat(draws, dims[dim] // parts).reshape([-1 if axis == dim else 1 for axis in range(len(dims))])
    return level


def gaussian(stream_key, extent, scale, limit, cuts=(), kind=jnp.bfloat16):
    values = scale * jax.random.normal(stream_key, extent, jnp.float32)
    if cuts:
        values = values * shard_levels(stream_key, extent, cuts, -0.22, 0.18)
    return jnp.clip(values, -limit, limit).astype(kind)


def setup_inputs(seed: int = 0) -> dict:
    key_of = jax.random.split(jax.random.key(seed), 16)
    return {
        "tokens": draw_tokens(jax.random.fold_in(key_of[15], 71), 0),
        "batch_order": jax.random.permutation(key_of[1], MB).astype(jnp.int32),
        "modulation": gaussian(key_of[2], (MB, 5, D), 0.5, 3.0, (), jnp.float32),
        "expand_weight": gaussian(key_of[3], (D, FF), D ** -0.5, 0.109375, ((0, 16), (1, 8))),
        "expand_bias": gaussian(key_of[4], (FF,), 0.5, 3.0, ((0, 8),), jnp.float32),
        "reduce_weight": gaussian(key_of[5], (FF, D), FF ** -0.5, 0.0546875, ((0, 8), (1, 16))),
        "reduce_bias": gaussian(key_of[6], (D,), 0.5, 3.0, ((0, 8),), jnp.float32),
        "patch_weight": gaussian(key_of[7], (D, PC), D ** -0.5, 0.109375, ((0, 8),), jnp.float32),
        "patch_bias": gaussian(key_of[8], (PC,), 0.5, 3.0, (), jnp.float32),
        "latent_kernel": gaussian(key_of[9], (3, 3, LC, VC), (9 * LC) ** -0.5, 0.5, (), jnp.float32),
        "latent_bias": gaussian(key_of[10], (VC,), 1.0, 4.0, (), jnp.float32),
        "group_gain": jnp.clip(1.0 + 0.18 * jax.random.normal(key_of[11], (VC,), jnp.float32), 0.1, 1.9),
        "group_shift": gaussian(key_of[12], (VC,), 0.5, 3.0, (), jnp.float32),
        "decode_kernel": gaussian(key_of[13], (3, 3, VC, VC), (9 * VC) ** -0.5, 0.09375, ((3, 2),)),
        "decode_bias": gaussian(key_of[14], (VC,), 0.5, 3.0, ((0, 2),), jnp.float32),
    }


EPSILON = 1e-06

def token_norm(values):
    row_mean = lax.optimization_barrier(jnp.mean(values, axis=-1, keepdims=True))
    row_var = lax.optimization_barrier(jnp.mean(values * values, axis=-1, keepdims=True)) - row_mean * row_mean
    return (values - row_mean) * lax.rsqrt(row_var + EPSILON)

def convolve(field_in, kernel):
    return lax.conv_general_dilated(field_in[None], kernel, (1, 1), 'SAME', dimension_numbers=('NHWC', 'HWIO', 'NHWC'), precision=lax.Precision.HIGHEST)[0]

def reference(tokens, batch_order, modulation, expand_weight, expand_bias, reduce_weight, reduce_bias, patch_weight, patch_bias, latent_kernel, latent_bias, group_gain, group_shift, decode_kernel, decode_bias):
    patch_rows = PR * N_ROW
    patch_cols = PCOLS * N_COL
    expand_full = expand_weight.astype(jnp.float32)
    reduce_full = reduce_weight.astype(jnp.float32)
    decode_full = decode_kernel.astype(jnp.float32)
    outputs = []
    for slot_index in range(MB):
        chosen = batch_order[slot_index]
        rows_in = tokens[chosen]
        factors = modulation[chosen]
        normed = (token_norm(rows_in) * (1.0 + factors[1]) + factors[0]).astype(jnp.bfloat16)
        hidden = jnp.dot(normed.astype(jnp.float32), expand_full, precision=lax.Precision.HIGHEST) + expand_bias
        hidden = jax.nn.gelu(hidden, approximate=True).astype(jnp.bfloat16)
        branch = jnp.dot(hidden.astype(jnp.float32), reduce_full, precision=lax.Precision.HIGHEST) + reduce_bias
        residual = rows_in + factors[2] * branch
        final_rows = token_norm(residual) * (1.0 + factors[4]) + factors[3]
        patches = jnp.dot(final_rows, patch_weight, precision=lax.Precision.HIGHEST) + patch_bias
        latent = patches / 0.3611 + 0.1159
        latent = latent.reshape(patch_rows, patch_cols, LC, 2, 2).transpose(0, 3, 1, 4, 2).reshape(2 * patch_rows, 2 * patch_cols, LC)
        activated = convolve(latent, latent_kernel) + latent_bias
        grouped = activated.reshape(2 * patch_rows, 2 * patch_cols, GROUPS, VC // GROUPS)
        group_mean = lax.optimization_barrier(jnp.mean(grouped, axis=(0, 1, 3), keepdims=True))
        group_variance = lax.optimization_barrier(jnp.mean(grouped * grouped, axis=(0, 1, 3), keepdims=True)) - group_mean * group_mean
        group_normalized = ((grouped - group_mean) * lax.rsqrt(group_variance + EPSILON)).reshape(activated.shape) * group_gain + group_shift
        group_normalized = jax.nn.silu(group_normalized).astype(jnp.bfloat16)
        upsampled = jnp.repeat(jnp.repeat(group_normalized, 2, axis=0), 2, axis=1)
        decoded = convolve(upsampled.astype(jnp.float32), decode_full) + decode_bias
        outputs.append(decoded)
    return jnp.stack(outputs)
```

```python
import functools

import jax
import jax.numpy as jnp
from jax import lax
from jax.experimental import pallas as pl
from jax.experimental.pallas import tpu as pltpu
from jax.sharding import PartitionSpec as P

MESH = pl.DeviceIdType.MESH
EPSILON = 1e-06
N_ROW = 16
N_COL = 8
CELLS = 64 * 64 * 16
LC = 16
MB = 4
PR = 2
PCOLS = 4
PC = 64


def phase_of(base, step):
    if base == 0:
        return [(1, 0), (0, 0), (1, 1)][step + 1]
    return [(0, 0), (1, 1), (0, 1)][step + 1]


def decoder_kernel(
    lat_ref,
    lk_ref,
    lb_ref,
    gain_ref,
    shift_ref,
    dk_ref,
    db_ref,
    out_ref,
    blocks,
    patches,
    weights,
    act,
    cells,
    products,
    col_stats,
    row_stats,
    halo_send,
    halo_recv,
    col_send,
    col_recv,
    row_send,
    row_recv,
):
    s = lax.axis_index("section")
    r = lax.axis_index("row")
    c = lax.axis_index("col")

    halo = []
    for ds in range(2):
        for dr in (-1, 0, 1):
            for dc in (-1, 0, 1):
                if (ds, dr, dc) != (0, 0, 0):
                    halo.append((ds, dr, dc))

    def place(ds, dr, dc):
        return (
            lax.rem(s + ds, 2),
            lax.rem(r + dr + N_ROW, N_ROW),
            lax.rem(c + dc + N_COL, N_COL),
        )

    barrier = pltpu.get_barrier_semaphore()
    greeted = 0
    for ds, dr, dc in halo:
        pl.semaphore_signal(barrier, inc=1, device_id=place(ds, dr, dc), device_id_type=MESH)
        greeted += 1
    for dc in range(2, N_COL - 1):
        pl.semaphore_signal(barrier, inc=1, device_id=place(0, 0, dc), device_id_type=MESH)
        greeted += 1
    for dr in range(2, N_ROW - 1):
        pl.semaphore_signal(barrier, inc=1, device_id=place(0, dr, 0), device_id_type=MESH)
        greeted += 1
    blocks[1, 1, s] = lat_ref[...]
    pl.semaphore_wait(barrier, greeted)

    copies = []
    for i, (ds, dr, dc) in enumerate(halo):
        copy = pltpu.make_async_remote_copy(
            src_ref=lat_ref,
            dst_ref=blocks.at[1 - dr, 1 - dc, s],
            send_sem=halo_send.at[ds, 1 - dr, 1 - dc],
            recv_sem=halo_recv.at[ds, 1 - dr, 1 - dc],
            device_id=place(ds, dr, dc),
            device_id_type=MESH,
        )
        copy.start()
        copies.append(copy)

    weights[...] = jnp.zeros_like(weights)
    for u in range(2):
        for v in range(2):
            for sa in range(2):
                for sb in range(2):
                    for a in range(2):
                        for b in range(2):
                            di = 2 * u + sa - 2 + a
                            dj = 2 * v + sb - 2 + b
                            if abs(di) <= 1 and abs(dj) <= 1:
                                row = ((u * 2 + v) * 2 + sa) * 2 + sb
                                tap = lk_ref[di + 1, dj + 1]
                                high = tap.astype(jnp.bfloat16)
                                low = (tap - high.astype(jnp.float32)).astype(jnp.bfloat16)
                                phase = 2 * a + b
                                rows = pl.ds(row * 16, 16)
                                lanes = pl.ds(phase * 512, 512)
                                weights[0, rows, lanes] = high
                                weights[1, rows, lanes] = low
    patches[...] = jnp.zeros_like(patches)

    for copy in copies:
        copy.wait()

    for ds in range(2):
        for dr in (-1, 0, 1):
            for dc in (-1, 0, 1):
                inside = (r + dr >= 0) & (r + dr < N_ROW) & (c + dc >= 0) & (c + dc < N_COL)
                keep = jnp.where(inside, 1.0, 0.0).astype(jnp.float32)
                block = blocks[dr + 1, dc + 1, ds][:, :64] * keep
                rows = {-1: ((1, 0),), 0: ((0, 1), (1, 2)), 1: ((0, 3),)}[dr]
                first, count, at = {-1: (3, 1, 0), 0: (0, 4, 1), 1: (0, 1, 5)}[dc]
                for mb in range(2):
                    for source, target in rows:
                        start = mb * 8 + source * 4 + first
                        patches[2 * ds + mb, target, at : at + count, :] = block[
                            start : start + count
                        ]

    slabs = [
        patches[:, u : u + 3, v : v + 8, :].reshape(96, 64) for u in range(2) for v in range(2)
    ]
    window = jnp.concatenate(slabs, axis=-1)
    high = window.astype(jnp.bfloat16)
    low = (window - high.astype(jnp.float32)).astype(jnp.bfloat16)
    both = jnp.concatenate([high, low], axis=0)

    jj = lax.broadcasted_iota(jnp.int32, (96, 1), 0) % 8
    ii = (lax.broadcasted_iota(jnp.int32, (96, 1), 0) // 8) % 3
    sums = jnp.zeros((4, 512), jnp.float32)
    squares = jnp.zeros((4, 512), jnp.float32)
    for a in range(2):
        for b in range(2):
            phase = 2 * a + b
            lanes = pl.ds(phase * 512, 512)
            first = jnp.dot(both, weights[0, :, lanes], preferred_element_type=jnp.float32)
            second = jnp.dot(high, weights[1, :, lanes], preferred_element_type=jnp.float32)
            value = first[:96] + (first[96:] + second) + lb_ref[...]
            act[phase] = value
            own = (ii >= a) & (ii < a + 2) & (jj >= b) & (jj < b + 4)
            masked = jnp.where(own, value, 0.0).reshape(4, 24, 512)
            sums += jnp.sum(masked, axis=1)
            squares += jnp.sum(masked * masked, axis=1)

    chan = lax.broadcasted_iota(jnp.int32, (512, 128), 0) // 16
    member = (chan == lax.broadcasted_iota(jnp.int32, (512, 128), 1)).astype(jnp.float32)
    chan_t = lax.broadcasted_iota(jnp.int32, (128, 512), 1) // 16
    member_t = (chan_t == lax.broadcasted_iota(jnp.int32, (128, 512), 0)).astype(jnp.float32)
    stats = jnp.dot(
        jnp.concatenate([sums, squares], axis=0),
        member,
        preferred_element_type=jnp.float32,
        precision=lax.Precision.HIGHEST,
    )

    col_stats[c] = stats
    copies = []
    for dc in range(1, N_COL):
        copy = pltpu.make_async_remote_copy(
            src_ref=col_stats.at[c],
            dst_ref=col_stats.at[c],
            send_sem=col_send.at[dc],
            recv_sem=col_recv.at[dc],
            device_id=place(0, 0, dc),
            device_id_type=MESH,
        )
        copy.start()
        copies.append(copy)
    for copy in copies:
        copy.wait()
    row_stats[r] = jnp.sum(col_stats[...], axis=0)
    copies = []
    for dr in range(1, N_ROW):
        copy = pltpu.make_async_remote_copy(
            src_ref=row_stats.at[r],
            dst_ref=row_stats.at[r],
            send_sem=row_send.at[dr],
            recv_sem=row_recv.at[dr],
            device_id=place(0, dr, 0),
            device_id_type=MESH,
        )
        copy.start()
        copies.append(copy)
    for copy in copies:
        copy.wait()
    total = jnp.sum(row_stats[...], axis=0) * (1.0 / CELLS)
    mean = total[:4]
    scale = lax.rsqrt(total[4:] - mean * mean + EPSILON)
    spread = jnp.dot(
        jnp.concatenate([mean, scale], axis=0),
        member_t,
        preferred_element_type=jnp.float32,
        precision=lax.Precision.HIGHEST,
    )

    for a in range(2):
        for b in range(2):
            phase = 2 * a + b
            line = 4 * r + 2 * ii - a
            across = 8 * c + 2 * jj - b
            inside = (line >= 0) & (line < 64) & (across >= 0) & (across < 64)
            parts = []
            for mb in range(4):
                value = act[phase, mb * 24 : mb * 24 + 24]
                value = (value - spread[mb : mb + 1]) * (
                    spread[4 + mb : 5 + mb] * gain_ref[...]
                ) + shift_ref[...]
                parts.append(value / (1.0 + jnp.exp(-value)))
            value = jnp.where(inside, jnp.concatenate(parts, axis=0), 0.0)
            cells[phase * 96 : phase * 96 + 96, :] = value.astype(jnp.bfloat16)

    for tap in range(9):
        value = jnp.dot(cells[...], dk_ref[tap], preferred_element_type=jnp.float32)
        products[tap] = value.reshape(4, 4, 3, 8, 256)

    for a in range(2):
        for b in range(2):
            for up in range(2):
                for left in range(2):
                    total = jnp.zeros((4, 2, 4, 256), jnp.float32) + db_ref[...]
                    for di in range(3):
                        row_phase, row_at = phase_of(a, (up + di - 1) // 2)
                        for dj in range(3):
                            col_phase, col_at = phase_of(b, (left + dj - 1) // 2)
                            total += products[
                                di * 3 + dj,
                                row_phase * 2 + col_phase,
                                :,
                                row_at : row_at + 2,
                                col_at : col_at + 4,
                                :,
                            ]
                    for mb in range(4):
                        for i in range(2):
                            for half in range(2):
                                out_ref[
                                    half,
                                    mb,
                                    4 * i + 2 * a + up,
                                    pl.ds(2 * b + left, 4, stride=4),
                                    :,
                                ] = total[mb, i, :, half * 128 : half * 128 + 128]


def decoder(latents, latent_kernel, latent_bias, gain, shift, decode_kernel, decode_bias):
    vmem = pl.BlockSpec(memory_space=pltpu.VMEM)
    out = pl.pallas_call(
        decoder_kernel,
        out_shape=jax.ShapeDtypeStruct((2, 4, 8, 16, 128), jnp.float32),
        in_specs=[vmem] * 7,
        out_specs=vmem,
        scratch_shapes=[
            pltpu.VMEM((3, 3, 2, 16, 128), jnp.float32),
            pltpu.VMEM((4, 4, 16, 64), jnp.float32),
            pltpu.VMEM((2, 256, 2048), jnp.bfloat16),
            pltpu.VMEM((4, 96, 512), jnp.float32),
            pltpu.VMEM((384, 512), jnp.bfloat16),
            pltpu.VMEM((9, 4, 4, 3, 8, 256), jnp.float32),
            pltpu.VMEM((8, 8, 128), jnp.float32),
            pltpu.VMEM((16, 8, 128), jnp.float32),
            pltpu.SemaphoreType.DMA((2, 3, 3)),
            pltpu.SemaphoreType.DMA((2, 3, 3)),
            pltpu.SemaphoreType.DMA((8,)),
            pltpu.SemaphoreType.DMA((8,)),
            pltpu.SemaphoreType.DMA((16,)),
            pltpu.SemaphoreType.DMA((16,)),
        ],
        compiler_params=pltpu.CompilerParams(
            collective_id=1, has_side_effects=True, vmem_limit_bytes=40 * 2**20
        ),
    )(
        latents,
        latent_kernel,
        latent_bias.reshape(1, 512),
        gain.reshape(1, 512),
        shift.reshape(1, 512),
        decode_kernel.reshape(9, 512, 256),
        decode_bias.reshape(1, 256),
    )
    return out.transpose(1, 2, 3, 0, 4).reshape(4, 8, 16, 256)


def shards(
    tokens,
    batch_order,
    modulation,
    expand_weight,
    expand_bias,
    reduce_weight,
    reduce_bias,
    patch_weight,
    patch_bias,
    latent_kernel,
    latent_bias,
    group_gain,
    group_shift,
    decode_kernel,
    decode_bias,
):
    col_count = lax.axis_size("col")
    row_count = lax.axis_size("row")
    col_place = lax.axis_index("col")
    section_place = lax.axis_index("section")
    tok_rows = tokens.shape[1]
    part_width = tokens.shape[2]
    full_width = part_width * col_count
    lat_rows = 2 * PR
    lat_cols = 2 * PCOLS
    rim_width = 1
    rim_edge = rim_width - 1
    expand_full, reduce_full = (
        lax.all_gather(expand_weight, "row", axis=0, tiled=True),
        lax.all_gather(reduce_weight, "row", axis=1, tiled=True),
    )

    def run_branch(normed_all):
        hidden = jnp.dot(normed_all, expand_full, preferred_element_type=jnp.float32) + expand_bias
        hidden = jax.nn.gelu(hidden, approximate=True).astype(jnp.bfloat16)
        return jnp.dot(hidden, reduce_full, preferred_element_type=jnp.float32)

    tower = []
    for section_step in range(MB):
        if True:
            chosen = batch_order[section_step]
            rows_in = lax.dynamic_index_in_dim(tokens, chosen, 0, keepdims=False)
            factors = lax.dynamic_index_in_dim(modulation, chosen, 0, keepdims=False)
            factors = lax.dynamic_slice_in_dim(factors, col_place * part_width, part_width, 1)
            row_sums, row_squares = lax.psum(
                (jnp.sum(rows_in, axis=1), jnp.sum(rows_in * rows_in, axis=1)), "col"
            )
            row_mean = (row_sums / full_width)[:, None]
            row_var = (row_squares / full_width)[:, None] - row_mean * row_mean
            normed = (
                (rows_in - row_mean) * lax.rsqrt(row_var + EPSILON) * (1.0 + factors[1])
                + factors[0]
            ).astype(jnp.bfloat16)
            tower_normed_all = lax.all_gather(normed, "col", axis=1, tiled=True)
            partial_branch = run_branch(tower_normed_all)
            branch = lax.psum_scatter(partial_branch, "col", scatter_dimension=1, tiled=True)
            residual = rows_in + factors[2] * (branch + reduce_bias)
            final_sums, final_squares = lax.psum(
                (jnp.sum(residual, axis=1), jnp.sum(residual * residual, axis=1)), "col"
            )
            final_mean = (final_sums / full_width)[:, None]
            final_var = (final_squares / full_width)[:, None] - final_mean * final_mean
            final_rows = (residual - final_mean) * lax.rsqrt(final_var + EPSILON) * (
                1.0 + factors[4]
            ) + factors[3]
            local_proj = jnp.dot(
                final_rows,
                patch_weight,
                preferred_element_type=jnp.float32,
                precision=lax.Precision.HIGHEST,
            )
            patches = lax.psum(local_proj, "col")
            patches = patches + patch_bias
            own_block = patches.reshape(PR, col_count, PCOLS, PC)
            tower.append(lax.dynamic_index_in_dim(own_block, col_place, 1, keepdims=False))
    latent = jnp.stack(tower) / 0.3611 + 0.1159
    latent = latent.reshape(MB, PR * PCOLS, LC, 4).transpose(0, 1, 3, 2).reshape(MB, PR * PCOLS, PC)
    latent = lax.dynamic_slice_in_dim(latent, 2 * section_place, 2, 0).reshape(16, PC)
    latent = jnp.pad(latent, ((0, 0), (0, 64)))
    return decoder(latent, latent_kernel, latent_bias, group_gain, group_shift, decode_kernel, decode_bias)


def solution(mesh):
    return jax.shard_map(
        shards,
        mesh=mesh,
        in_specs=(
            P(None, "row", "col"),
            P(),
            P(),
            P("row", "col"),
            P("col"),
            P("col", "row"),
            P("col"),
            P("col", None),
            P(),
            P(),
            P(),
            P(),
            P(),
            P(None, None, None, "section"),
            P("section"),
        ),
        out_specs=P(None, "row", "col", "section"),
        check_vma=False,
    )
```

```python
import functools

import jax
import jax.numpy as jnp
from jax import lax
from jax.experimental import pallas as pl
from jax.experimental.pallas import tpu as pltpu
from jax.sharding import PartitionSpec as P

MESH = pl.DeviceIdType.MESH
EPSILON = 1e-06
N_ROW = 16
N_COL = 8
CELLS = 64 * 64 * 16


def phase_of(base, step):
    if base == 0:
        return [(1, 0), (0, 0), (1, 1)][step + 1]
    return [(0, 0), (1, 1), (0, 1)][step + 1]


def decoder_kernel(
    lat_ref,
    lk_ref,
    lb_ref,
    gain_ref,
    shift_ref,
    dk_ref,
    db_ref,
    out_ref,
    blocks,
    patches,
    weights,
    act,
    cells,
    products,
    col_stats,
    row_stats,
    halo_send,
    halo_recv,
    col_send,
    col_recv,
    row_send,
    row_recv,
):
    s = lax.axis_index("section")
    r = lax.axis_index("row")
    c = lax.axis_index("col")

    halo = []
    for ds in range(2):
        for dr in (-1, 0, 1):
            for dc in (-1, 0, 1):
                if (ds, dr, dc) != (0, 0, 0):
                    halo.append((ds, dr, dc))

    def place(ds, dr, dc):
        return (
            lax.rem(s + ds, 2),
            lax.rem(r + dr + N_ROW, N_ROW),
            lax.rem(c + dc + N_COL, N_COL),
        )

    barrier = pltpu.get_barrier_semaphore()
    greeted = 0
    for ds, dr, dc in halo:
        pl.semaphore_signal(barrier, inc=1, device_id=place(ds, dr, dc), device_id_type=MESH)
        greeted += 1
    for dc in range(2, N_COL - 1):
        pl.semaphore_signal(barrier, inc=1, device_id=place(0, 0, dc), device_id_type=MESH)
        greeted += 1
    for dr in range(2, N_ROW - 1):
        pl.semaphore_signal(barrier, inc=1, device_id=place(0, dr, 0), device_id_type=MESH)
        greeted += 1
    blocks[1, 1, s] = lat_ref[...]
    pl.semaphore_wait(barrier, greeted)

    copies = []
    for i, (ds, dr, dc) in enumerate(halo):
        copy = pltpu.make_async_remote_copy(
            src_ref=lat_ref,
            dst_ref=blocks.at[1 - dr, 1 - dc, s],
            send_sem=halo_send.at[ds, 1 - dr, 1 - dc],
            recv_sem=halo_recv.at[ds, 1 - dr, 1 - dc],
            device_id=place(ds, dr, dc),
            device_id_type=MESH,
        )
        copy.start()
        copies.append(copy)

    weights[...] = jnp.zeros_like(weights)
    for u in range(2):
        for v in range(2):
            for sa in range(2):
                for sb in range(2):
                    for a in range(2):
                        for b in range(2):
                            di = 2 * u + sa - 2 + a
                            dj = 2 * v + sb - 2 + b
                            if abs(di) <= 1 and abs(dj) <= 1:
                                row = ((u * 2 + v) * 2 + sa) * 2 + sb
                                tap = lk_ref[di + 1, dj + 1]
                                high = tap.astype(jnp.bfloat16)
                                low = (tap - high.astype(jnp.float32)).astype(jnp.bfloat16)
                                phase = 2 * a + b
                                rows = pl.ds(row * 16, 16)
                                lanes = pl.ds(phase * 512, 512)
                                weights[0, rows, lanes] = high
                                weights[1, rows, lanes] = low
    patches[...] = jnp.zeros_like(patches)

    for copy in copies:
        copy.wait()

    for ds in range(2):
        for dr in (-1, 0, 1):
            for dc in (-1, 0, 1):
                inside = (r + dr >= 0) & (r + dr < N_ROW) & (c + dc >= 0) & (c + dc < N_COL)
                keep = jnp.where(inside, 1.0, 0.0).astype(jnp.float32)
                block = blocks[dr + 1, dc + 1, ds][:, :64] * keep
                rows = {-1: ((1, 0),), 0: ((0, 1), (1, 2)), 1: ((0, 3),)}[dr]
                first, count, at = {-1: (3, 1, 0), 0: (0, 4, 1), 1: (0, 1, 5)}[dc]
                for mb in range(2):
                    for source, target in rows:
                        start = mb * 8 + source * 4 + first
                        patches[2 * ds + mb, target, at : at + count, :] = block[
                            start : start + count
                        ]

    slabs = [
        patches[:, u : u + 3, v : v + 8, :].reshape(96, 64) for u in range(2) for v in range(2)
    ]
    window = jnp.concatenate(slabs, axis=-1)
    high = window.astype(jnp.bfloat16)
    low = (window - high.astype(jnp.float32)).astype(jnp.bfloat16)
    both = jnp.concatenate([high, low], axis=0)

    jj = lax.broadcasted_iota(jnp.int32, (96, 1), 0) % 8
    ii = (lax.broadcasted_iota(jnp.int32, (96, 1), 0) // 8) % 3
    sums = jnp.zeros((4, 512), jnp.float32)
    squares = jnp.zeros((4, 512), jnp.float32)
    for a in range(2):
        for b in range(2):
            phase = 2 * a + b
            lanes = pl.ds(phase * 512, 512)
            first = jnp.dot(both, weights[0, :, lanes], preferred_element_type=jnp.float32)
            second = jnp.dot(high, weights[1, :, lanes], preferred_element_type=jnp.float32)
            value = first[:96] + (first[96:] + second) + lb_ref[...]
            act[phase] = value
            own = (ii >= a) & (ii < a + 2) & (jj >= b) & (jj < b + 4)
            masked = jnp.where(own, value, 0.0).reshape(4, 24, 512)
            sums += jnp.sum(masked, axis=1)
            squares += jnp.sum(masked * masked, axis=1)

    chan = lax.broadcasted_iota(jnp.int32, (512, 128), 0) // 16
    member = (chan == lax.broadcasted_iota(jnp.int32, (512, 128), 1)).astype(jnp.float32)
    chan_t = lax.broadcasted_iota(jnp.int32, (128, 512), 1) // 16
    member_t = (chan_t == lax.broadcasted_iota(jnp.int32, (128, 512), 0)).astype(jnp.float32)
    stats = jnp.dot(
        jnp.concatenate([sums, squares], axis=0),
        member,
        preferred_element_type=jnp.float32,
        precision=lax.Precision.HIGHEST,
    )

    col_stats[c] = stats
    copies = []
    for dc in range(1, N_COL):
        copy = pltpu.make_async_remote_copy(
            src_ref=col_stats.at[c],
            dst_ref=col_stats.at[c],
            send_sem=col_send.at[dc],
            recv_sem=col_recv.at[dc],
            device_id=place(0, 0, dc),
            device_id_type=MESH,
        )
        copy.start()
        copies.append(copy)
    for copy in copies:
        copy.wait()
    row_stats[r] = jnp.sum(col_stats[...], axis=0)
    copies = []
    for dr in range(1, N_ROW):
        copy = pltpu.make_async_remote_copy(
            src_ref=row_stats.at[r],
            dst_ref=row_stats.at[r],
            send_sem=row_send.at[dr],
            recv_sem=row_recv.at[dr],
            device_id=place(0, dr, 0),
            device_id_type=MESH,
        )
        copy.start()
        copies.append(copy)
    for copy in copies:
        copy.wait()
    total = jnp.sum(row_stats[...], axis=0) * (1.0 / CELLS)
    mean = total[:4]
    scale = lax.rsqrt(total[4:] - mean * mean + EPSILON)
    spread = jnp.dot(
        jnp.concatenate([mean, scale], axis=0),
        member_t,
        preferred_element_type=jnp.float32,
        precision=lax.Precision.HIGHEST,
    )

    for a in range(2):
        for b in range(2):
            phase = 2 * a + b
            line = 4 * r + 2 * ii - a
            across = 8 * c + 2 * jj - b
            inside = (line >= 0) & (line < 64) & (across >= 0) & (across < 64)
            parts = []
            for mb in range(4):
                value = act[phase, mb * 24 : mb * 24 + 24]
                value = (value - spread[mb : mb + 1]) * (
                    spread[4 + mb : 5 + mb] * gain_ref[...]
                ) + shift_ref[...]
                parts.append(value / (1.0 + jnp.exp(-value)))
            value = jnp.where(inside, jnp.concatenate(parts, axis=0), 0.0)
            cells[phase * 96 : phase * 96 + 96, :] = value.astype(jnp.bfloat16)

    for tap in range(9):
        value = jnp.dot(cells[...], dk_ref[tap], preferred_element_type=jnp.float32)
        products[tap] = value.reshape(4, 4, 3, 8, 256)

    for a in range(2):
        for b in range(2):
            for up in range(2):
                for left in range(2):
                    total = jnp.zeros((4, 2, 4, 256), jnp.float32) + db_ref[...]
                    for di in range(3):
                        row_phase, row_at = phase_of(a, (up + di - 1) // 2)
                        for dj in range(3):
                            col_phase, col_at = phase_of(b, (left + dj - 1) // 2)
                            total += products[
                                di * 3 + dj,
                                row_phase * 2 + col_phase,
                                :,
                                row_at : row_at + 2,
                                col_at : col_at + 4,
                                :,
                            ]
                    for mb in range(4):
                        for i in range(2):
                            for half in range(2):
                                out_ref[
                                    half,
                                    mb,
                                    4 * i + 2 * a + up,
                                    pl.ds(2 * b + left, 4, stride=4),
                                    :,
                                ] = total[mb, i, :, half * 128 : half * 128 + 128]


def decoder(latents, latent_kernel, latent_bias, gain, shift, decode_kernel, decode_bias):
    vmem = pl.BlockSpec(memory_space=pltpu.VMEM)
    out = pl.pallas_call(
        decoder_kernel,
        out_shape=jax.ShapeDtypeStruct((2, 4, 8, 16, 128), jnp.float32),
        in_specs=[vmem] * 7,
        out_specs=vmem,
        scratch_shapes=[
            pltpu.VMEM((3, 3, 2, 16, 128), jnp.float32),
            pltpu.VMEM((4, 4, 16, 64), jnp.float32),
            pltpu.VMEM((2, 256, 2048), jnp.bfloat16),
            pltpu.VMEM((4, 96, 512), jnp.float32),
            pltpu.VMEM((384, 512), jnp.bfloat16),
            pltpu.VMEM((9, 4, 4, 3, 8, 256), jnp.float32),
            pltpu.VMEM((8, 8, 128), jnp.float32),
            pltpu.VMEM((16, 8, 128), jnp.float32),
            pltpu.SemaphoreType.DMA((2, 3, 3)),
            pltpu.SemaphoreType.DMA((2, 3, 3)),
            pltpu.SemaphoreType.DMA((8,)),
            pltpu.SemaphoreType.DMA((8,)),
            pltpu.SemaphoreType.DMA((16,)),
            pltpu.SemaphoreType.DMA((16,)),
        ],
        compiler_params=pltpu.CompilerParams(
            collective_id=1, has_side_effects=True, vmem_limit_bytes=40 * 2**20
        ),
    )(
        latents,
        latent_kernel,
        latent_bias.reshape(1, 512),
        gain.reshape(1, 512),
        shift.reshape(1, 512),
        decode_kernel.reshape(9, 512, 256),
        decode_bias.reshape(1, 256),
    )
    return out.transpose(1, 2, 3, 0, 4).reshape(4, 8, 16, 256)


WIDTH = 3072
BLOCK = 384
PIECE = 192
OFFSETS = (0, -1, 1, -2, 2, -3, 3, 4)


def tower_kernel(
    tok_ref,
    first_ref,
    final_ref,
    expand_ref,
    reduce_ref,
    expand_bias_ref,
    reduce_bias_ref,
    patch_ref,
    patch_bias_ref,
    out_ref,
    normed,
    weights,
    total,
    hidden,
    based,
    rows_in,
    patch_all,
    stats,
    sib_out,
    sib_in,
    kept,
    outgoing,
    incoming,
    residual,
    local_sem,
    partner_send,
    partner_recv,
    ring_send,
    ring_recv,
    stat_send,
    stat_recv,
    base_send,
    base_recv,
    patch_send,
    patch_recv,
    tok_send,
    tok_recv,
    fwd_send,
    fwd_recv,
    sib_send,
    sib_recv,
    sum_send,
    sum_recv,
):
    s = lax.axis_index("section")
    r = lax.axis_index("row")
    c = lax.axis_index("col")
    z, yh = r // 2, r % 2
    x, k = c // 2, c % 2
    quarter = 2 * yh + s
    sibling = (s, r, 2 * x + 1 - k)
    partner = (1 - s, 2 * z + 1 - yh, c)

    def ring_place(step):
        return (s, 2 * lax.rem(z + step + 8, 8) + yh, c)

    def col_place(step):
        return (s, r, lax.rem(c + step, 8))

    def plane_place(dy, ds, dx):
        return (lax.rem(s + ds, 2), 2 * z + lax.rem(yh + dy, 2), 2 * lax.rem(x + dx, 4) + k)

    def send(source, target, send_sem, recv_sem, place):
        copy = pltpu.make_async_remote_copy(
            src_ref=source,
            dst_ref=target,
            send_sem=send_sem,
            recv_sem=recv_sem,
            device_id=place,
            device_id_type=MESH,
        )
        copy.start()
        return copy

    sent = []
    own_lanes = pl.ds(pl.multiple_of(quarter * BLOCK, BLOCK), BLOCK)
    other_lanes = pl.ds(pl.multiple_of((3 - quarter) * BLOCK, BLOCK), BLOCK)
    sources = (expand_ref, reduce_ref)
    local = []
    for e in range(2):
        copy = pltpu.make_async_copy(
            sources[e].at[:, own_lanes], weights.at[z, e, yh], local_sem.at[e]
        )
        copy.start()
        local.append(copy)

    barrier = pltpu.get_barrier_semaphore()
    greet = [ring_place(1), ring_place(-1)]
    greet += [col_place(step) for step in range(1, 8)]
    for dy, ds in ((0, 1), (1, 0), (1, 1)):
        greet += [plane_place(dy, ds, dx) for dx in range(4)]
    for place in greet:
        pl.semaphore_signal(barrier, inc=1, device_id=place, device_id_type=MESH)
    pl.semaphore_wait(barrier, len(greet))

    from_partner = []
    for e in range(2):
        from_partner.append(
            send(
                sources[e].at[:, other_lanes],
                weights.at[z, e, yh],
                partner_send.at[e],
                partner_recv.at[e],
                partner,
            )
        )
    for copy in local:
        copy.wait()

    ring = {}
    arrived = set()

    def ensure(e, o, way, d):
        if (e, o, way, d) not in arrived:
            ring[e, o, way, d].wait_recv()
            arrived.add((e, o, way, d))

    def reach(o, way):
        return 4 if (o == 0) == (way == 1) else 3

    def ring_step(e, d, units=(0, 1)):
        for o in units:
            half = lax.rem(yh + o, 2)
            for way in (1, -1):
                if d > reach(o, way):
                    continue
                if d > 1:
                    ensure(e, o, way, d - 1)
                held = weights.at[lax.rem(z - way * (d - 1) + 8, 8), e, half]
                index = (1 - way) // 2
                ring[e, o, way, d] = send(
                    held,
                    held,
                    ring_send.at[e, o, index, d - 1],
                    ring_recv.at[e, o, index, d - 1],
                    ring_place(way),
                )

    def arrive(e, d):
        for o in range(2):
            for way in (1, -1):
                if d <= reach(o, way):
                    ensure(e, o, way, d)

    ring_step(0, 1, (0,))

    tok = tok_ref[...].reshape(256, BLOCK)
    lane = lax.broadcasted_iota(jnp.int32, (256, 128), 1)
    token_sums = jnp.sum(tok, axis=1, keepdims=True)
    token_squares = jnp.sum(tok * tok, axis=1, keepdims=True)
    table = jnp.where(lane == 0, token_sums, jnp.where(lane == 1, token_squares, 0.0))
    stats[c] = table.T[:8]
    stat_copies = [
        send(stats.at[c], stats.at[c], stat_send.at[d], stat_recv.at[d], col_place(d))
        for d in range(1, 8)
    ]
    sent += stat_copies

    from_partner[0].wait_recv()
    ring_step(0, 1, (1,))

    for core in range(2):
        for group in range(8):
            rows = pl.ds(group * 16, 16)
            part = tok_ref[core, rows, :].reshape(2, 8, BLOCK)
            part = part + first_ref[2, group // 4] * reduce_bias_ref[...]
            based[core, rows, :] = part.reshape(16, BLOCK)

    for copy in stat_copies:
        copy.wait_recv()
    table = jnp.concatenate(
        [jnp.sum(stats[...], axis=0), jnp.zeros((120, 256), jnp.float32)], axis=0
    ).T
    token_mean = table[:, 0:1] * (1.0 / WIDTH)
    token_scale = lax.rsqrt(table[:, 1:2] * (1.0 / WIDTH) - token_mean * token_mean + EPSILON)
    plain = (tok - token_mean) * token_scale
    for core in range(2):
        for group in range(8):
            start = core * 128 + group * 16
            part = plain[start : start + 16].reshape(2, 8, BLOCK)
            part = part * (1.0 + first_ref[1, group // 4]) + first_ref[0, group // 4]
            normed[c, core, yh, pl.ds(group * 16, 16), :] = part.reshape(16, BLOCK).astype(
                jnp.bfloat16
            )

    mine = normed.at[c, :, yh]
    tok_copies = {}
    for dy, dx in ((1, 0), (0, 1), (0, 3), (1, 1), (1, 3), (0, 2), (1, 2)):
        tok_copies[dy, dx] = send(
            mine, mine, tok_send.at[dy, dx], tok_recv.at[dy, dx], plane_place(dy, dy, dx)
        )
    tok_copies[0, 0] = send(mine, mine, tok_send.at[0, 0], tok_recv.at[0, 0], sibling)
    sent += tok_copies.values()

    base_copies = []
    for d in range(1, 8):
        target = lax.rem(c + d, 8)
        rows = pl.ds(pl.multiple_of((s * 4 + target // 2) * 16, 16), 16)
        base_copies.append(
            send(
                based.at[target % 2, rows, :],
                rows_in.at[c],
                base_send.at[d],
                base_recv.at[d],
                col_place(d),
            )
        )
    sent += base_copies
    own_rows = pl.ds(pl.multiple_of((s * 4 + x) * 16, 16), 16)
    rows_in[c] = based[k, own_rows, :]

    ring_step(0, 2)

    forwards = []

    def forward(dy, dx):
        tok_copies[dy, dx].wait_recv()
        piece = normed.at[2 * lax.rem(x - dx + 4, 4) + k, :, lax.rem(yh + dy, 2)]
        forwards.append(send(piece, piece, fwd_send.at[dy, dx], fwd_recv.at[dy, dx], sibling))

    for dy, dx in ((1, 0), (0, 1), (0, 3)):
        forward(dy, dx)
    ring_step(0, 3)
    for dy, dx in ((1, 1), (1, 3), (0, 2), (1, 2)):
        forward(dy, dx)
    from_partner[1].wait_recv()
    ring_step(1, 1)
    sent += forwards

    high = patch_ref[...].astype(jnp.bfloat16)
    low = (patch_ref[...] - high.astype(jnp.float32)).astype(jnp.bfloat16)
    patch_all[c] = jnp.concatenate([high, low], axis=1)
    patch_copies = [
        send(patch_all.at[c], patch_all.at[c], patch_send.at[d], patch_recv.at[d], col_place(d))
        for d in range(1, 8)
    ]
    sent += patch_copies

    tok_copies[0, 0].wait_recv()
    for copy in forwards:
        copy.wait_recv()

    def expand(offset):
        at = lax.rem(z + offset + 8, 8)
        value = jnp.dot(
            normed[at].reshape(512, BLOCK),
            weights[at, 0].reshape(BLOCK, BLOCK),
            preferred_element_type=jnp.float32,
        )
        if offset == 0:
            total[...] = value
        else:
            total[...] += value

    for offset in OFFSETS[:5]:
        if offset in (-2, 2):
            arrive(0, 2)
        expand(offset)
    ring_step(0, 4)
    ring_step(1, 2)
    arrive(0, 3)
    expand(-3)
    expand(3)
    arrive(0, 4)
    expand(4)
    value = total[...] + expand_bias_ref[...]
    inner = 0.7978845608028654 * (value + 0.044715 * (value * value * value))
    value = 0.5 * value * (1.0 + jnp.tanh(inner))
    hidden[...] = value.astype(jnp.bfloat16).reshape(2, 256, BLOCK)
    ring_step(1, 3)

    sib_copies = []

    def contract(g):
        for slot in (2 * g, 2 * g + 1):
            at = lax.rem(z + OFFSETS[slot] + 8, 8)
            right = weights[at, 1].reshape(BLOCK, BLOCK)
            away = lax.dot_general(
                hidden[1 - k], right, (((1,), (1,)), ((), ())), preferred_element_type=jnp.float32
            )
            sib_out[slot] = away.astype(jnp.bfloat16)
            sib_copies.append(
                send(
                    sib_out.at[slot], sib_in.at[slot], sib_send.at[slot], sib_recv.at[slot], sibling
                )
            )
            kept[slot] = lax.dot_general(
                hidden[k], right, (((1,), (1,)), ((), ())), preferred_element_type=jnp.float32
            )

    m_own = yh * 8 + s * 4 + x
    sum_copies = {}

    def scatter(g):
        for slot in (2 * g, 2 * g + 1):
            sib_copies[slot].wait_recv()
            value = kept[slot] + sib_in[slot].astype(jnp.float32)
            outgoing[slot] = value.astype(jnp.bfloat16).reshape(16, 16, BLOCK)
        pair = pl.ds(2 * g, 2)
        for dy in range(2):
            for ds in range(2):
                for dx in range(4):
                    if (dy, ds, dx) == (0, 0, 0):
                        continue
                    place = plane_place(dy, ds, dx)
                    m_there = lax.rem(yh + dy, 2) * 8 + place[0] * 4 + lax.rem(x + dx, 4)
                    m = dy * 8 + ds * 4 + dx
                    sum_copies[g, m] = send(
                        outgoing.at[pair, m_there],
                        incoming.at[pair, m_own],
                        sum_send.at[g, m],
                        sum_recv.at[g, m],
                        place,
                    )
        incoming[pair, m_own] = outgoing[pair, m_own]

    contract(0)
    ring_step(1, 4)
    arrive(1, 2)
    contract(1)
    scatter(0)
    arrive(1, 3)
    contract(2)
    scatter(1)
    arrive(1, 4)
    contract(3)
    scatter(2)
    scatter(3)

    for copy in base_copies:
        copy.wait_recv()
    row_sums = jnp.zeros((2, 8, 1), jnp.float32)
    row_squares = jnp.zeros((2, 8, 1), jnp.float32)
    for g in range(4):
        for m in range(1, 16):
            sum_copies[g, m].wait_recv()
        for slot in (2 * g, 2 * g + 1):
            at = lax.rem(z + OFFSETS[slot] + 8, 8)
            branch = jnp.sum(incoming[slot].astype(jnp.float32), axis=0)
            value = rows_in[at].reshape(2, 8, BLOCK) + final_ref[0, at] * branch.reshape(
                2, 8, BLOCK
            )
            residual[slot] = value
            row_sums += jnp.sum(value, axis=2, keepdims=True)
            row_squares += jnp.sum(value * value, axis=2, keepdims=True)
    row_mean = row_sums * (1.0 / WIDTH)
    row_scale = lax.rsqrt(row_squares * (1.0 / WIDTH) - row_mean * row_mean + EPSILON)
    for copy in patch_copies:
        copy.wait_recv()
    projected = jnp.zeros((32, 128), jnp.float32)
    for slot in range(8):
        at = lax.rem(z + OFFSETS[slot] + 8, 8)
        value = (residual[slot] - row_mean) * row_scale * (1.0 + final_ref[2, at]) + final_ref[
            1, at
        ]
        value = value.reshape(16, BLOCK)
        high = value.astype(jnp.bfloat16)
        low = (value - high.astype(jnp.float32)).astype(jnp.bfloat16)
        projected += jnp.dot(
            jnp.concatenate([high, low], axis=0),
            patch_all[at],
            preferred_element_type=jnp.float32,
        )
    patch = projected[:16, :64] + (projected[16:, :64] + projected[:16, 64:])
    latent = (patch + patch_bias_ref[...]) / 0.3611 + 0.1159
    out_ref[...] = jnp.concatenate([latent, jnp.zeros((16, 64), jnp.float32)], axis=1)

    for copy in from_partner:
        copy.wait_send()
    for copy in ring.values():
        copy.wait_send()
    for copy in sent:
        copy.wait_send()
    for copy in sib_copies:
        copy.wait_send()
    for copy in sum_copies.values():
        copy.wait_send()


def tower(tok, first, final, expand, reduce_t, expand_bias, reduce_bias, patch, patch_bias):
    vmem = pl.BlockSpec(memory_space=pltpu.VMEM)
    bf16, f32 = jnp.bfloat16, jnp.float32
    dma = pltpu.SemaphoreType.DMA
    return pl.pallas_call(
        tower_kernel,
        out_shape=jax.ShapeDtypeStruct((16, 128), f32),
        in_specs=[vmem] * 9,
        out_specs=vmem,
        scratch_shapes=[
            pltpu.VMEM((8, 2, 2, 128, BLOCK), bf16),
            pltpu.VMEM((8, 2, 2, PIECE, BLOCK), bf16),
            pltpu.VMEM((512, BLOCK), f32),
            pltpu.VMEM((2, 256, BLOCK), bf16),
            pltpu.VMEM((2, 128, BLOCK), f32),
            pltpu.VMEM((8, 16, BLOCK), f32),
            pltpu.VMEM((8, BLOCK, 128), bf16),
            pltpu.VMEM((8, 8, 256), f32),
            pltpu.VMEM((8, 256, BLOCK), bf16),
            pltpu.VMEM((8, 256, BLOCK), bf16),
            pltpu.VMEM((8, 256, BLOCK), f32),
            pltpu.VMEM((8, 16, 16, BLOCK), bf16),
            pltpu.VMEM((8, 16, 16, BLOCK), bf16),
            pltpu.VMEM((8, 2, 8, BLOCK), f32),
            dma((2,)),
            dma((2,)),
            dma((2,)),
            dma((2, 2, 2, 4)),
            dma((2, 2, 2, 4)),
            dma((8,)),
            dma((8,)),
            dma((8,)),
            dma((8,)),
            dma((8,)),
            dma((8,)),
            dma((2, 4)),
            dma((2, 4)),
            dma((2, 4)),
            dma((2, 4)),
            dma((8,)),
            dma((8,)),
            dma((4, 16)),
            dma((4, 16)),
        ],
        compiler_params=pltpu.CompilerParams(
            collective_id=0, has_side_effects=True, vmem_limit_bytes=48 * 2**20
        ),
    )(tok, first, final, expand, reduce_t, expand_bias, reduce_bias, patch, patch_bias)


def shards(
    tokens,
    batch_order,
    modulation,
    expand_weight,
    expand_bias,
    reduce_weight,
    reduce_bias,
    patch_weight,
    patch_bias,
    latent_kernel,
    latent_bias,
    group_gain,
    group_shift,
    decode_kernel,
    decode_bias,
):
    s = lax.axis_index("section")
    r = lax.axis_index("row")
    c = lax.axis_index("col")
    quarter = 2 * (r % 2) + s
    tok = jnp.take(tokens, batch_order, axis=0)
    tok = tok.reshape(2, 2, 2, 4, 2, 4, BLOCK).transpose(4, 0, 3, 1, 2, 5, 6).reshape(2, 128, BLOCK)
    factors = jnp.take(modulation, batch_order, axis=0)
    first = lax.dynamic_slice_in_dim(factors, c * BLOCK, BLOCK, 2)[:, :3]
    first = first.transpose(1, 0, 2).reshape(3, 2, 2, 1, BLOCK)
    final = lax.dynamic_slice_in_dim(factors, 2 * s, 2, 0)[:, 2:]
    final = final.reshape(2, 3, 8, 1, BLOCK).transpose(1, 2, 0, 3, 4)
    patch = patch_weight.reshape(BLOCK, 16, 4).transpose(0, 2, 1).reshape(BLOCK, 64)
    latents = tower(
        tok,
        first,
        final,
        expand_weight,
        reduce_weight.T,
        lax.dynamic_slice_in_dim(expand_bias, quarter * BLOCK, BLOCK, 0).reshape(1, BLOCK),
        reduce_bias.reshape(1, BLOCK),
        patch,
        patch_bias.reshape(16, 4).T.reshape(1, 64),
    )
    return decoder(
        latents, latent_kernel, latent_bias, group_gain, group_shift, decode_kernel, decode_bias
    )


def solution(mesh):
    return jax.shard_map(
        shards,
        mesh=mesh,
        in_specs=(
            P(None, "row", "col"),
            P(),
            P(),
            P("row", "col"),
            P("col"),
            P("col", "row"),
            P("col"),
            P("col", None),
            P(),
            P(),
            P(),
            P(),
            P(),
            P(None, None, None, "section"),
            P("section"),
        ),
        out_specs=P(None, "row", "col", "section"),
        check_vma=False,
    )
```

```python
from types import SimpleNamespace

import jax
import jax.numpy as jnp
from jax import lax
from jax.experimental import pallas as pl
from jax.experimental.pallas import tpu as pltpu
from jax.sharding import PartitionSpec as P

MESH = pl.DeviceIdType.MESH
EPSILON = 1e-06
N_ROW = 16
N_COL = 8
CELLS = 64 * 64 * 16
WIDTH = 3072
BLOCK = 384
PIECE = 192
GROUPS = ((0, -1, 1), (-2, 2), (-3, 3), (4,))
OFFSETS = (0, -1, 1, -2, 2, -3, 3, 4)
BF16, F32 = jnp.bfloat16, jnp.float32
DMA = pltpu.SemaphoreType.DMA
INPUTS = {
    "tokens": pl.ANY,
    "order": pltpu.SMEM,
    "modulation": pl.ANY,
    "expand": pl.ANY,
    "expand_bias": pltpu.VMEM,
    "reduce": pl.ANY,
    "reduce_bias": pltpu.VMEM,
    "patch": pltpu.VMEM,
    "patch_bias": pltpu.VMEM,
    "latent_kernel": pl.ANY,
    "latent_bias": pltpu.VMEM,
    "gain": pltpu.VMEM,
    "shift": pltpu.VMEM,
    "decode_kernel": pl.ANY,
    "decode_bias": pltpu.VMEM,
}
SCRATCH = {
    "tokens_in": pltpu.VMEM((4, 64, BLOCK), F32),
    "factors": pltpu.VMEM((5, 4, WIDTH), F32),
    "latent_in": pltpu.VMEM((3, 3, 16, 512), F32),
    "decode_in": pltpu.VMEM((9, 512, 256), BF16),
    "tok": pltpu.VMEM((2, 128, BLOCK), F32),
    "first": pltpu.VMEM((3, 2, 2, 1, BLOCK), F32),
    "final": pltpu.VMEM((3, 8, 2, 1, BLOCK), F32),
    "normed": pltpu.VMEM((8, 2, 2, 128, BLOCK), BF16),
    "weights": pltpu.VMEM((8, 2, 2, PIECE, BLOCK), BF16),
    "total": pltpu.VMEM((512, BLOCK), F32),
    "hidden": pltpu.VMEM((2, 256, BLOCK), BF16),
    "based": pltpu.VMEM((2, 128, BLOCK), F32),
    "rows_in": pltpu.VMEM((8, 16, BLOCK), F32),
    "patch_all": pltpu.VMEM((8, BLOCK, 128), BF16),
    "stats": pltpu.VMEM((8, 8, 256), F32),
    "sib_out": pltpu.VMEM((8, 256, BLOCK), BF16),
    "sib_in": pltpu.VMEM((8, 256, BLOCK), BF16),
    "kept": pltpu.VMEM((8, 256, BLOCK), F32),
    "outgoing": pltpu.VMEM((8, 16, 16, BLOCK), BF16),
    "incoming": pltpu.VMEM((8, 16, 16, BLOCK), BF16),
    "residual": pltpu.VMEM((8, 2, 8, BLOCK), F32),
    "latents": pltpu.VMEM((16, 128), F32),
    "blocks": pltpu.VMEM((3, 3, 2, 16, 128), F32),
    "patches": pltpu.VMEM((4, 4, 16, 64), F32),
    "taps": pltpu.VMEM((2, 256, 2048), BF16),
    "act": pltpu.VMEM((4, 96, 512), F32),
    "cells": pltpu.VMEM((384, 512), BF16),
    "products": pltpu.VMEM((9, 4, 4, 3, 8, 256), F32),
    "col_stats": pltpu.VMEM((8, 8, 128), F32),
    "row_stats": pltpu.VMEM((16, 8, 128), F32),
    "load_sem": DMA((8,)),
    "partner_send": DMA((2,)),
    "partner_recv": DMA((2,)),
    "ring_send": DMA((2, 2, 2, 4)),
    "ring_recv": DMA((2, 2, 2, 4)),
    "stat_send": DMA((8,)),
    "stat_recv": DMA((8,)),
    "base_send": DMA((8,)),
    "base_recv": DMA((8,)),
    "patch_send": DMA((8,)),
    "patch_recv": DMA((8,)),
    "tok_send": DMA((2, 4)),
    "tok_recv": DMA((2, 4)),
    "fwd_send": DMA((2, 4)),
    "fwd_recv": DMA((2, 4)),
    "sib_send": DMA((8,)),
    "sib_recv": DMA((8,)),
    "sum_send": DMA((4, 16)),
    "sum_recv": DMA((4, 16)),
    "halo_send": DMA((2, 3, 3)),
    "halo_recv": DMA((2, 3, 3)),
    "col_send": DMA((8,)),
    "col_recv": DMA((8,)),
    "row_send": DMA((16,)),
    "row_recv": DMA((16,)),
}


def phase_of(base, step):
    if base == 0:
        return [(1, 0), (0, 0), (1, 1)][step + 1]
    return [(0, 0), (1, 1), (0, 1)][step + 1]


def program_kernel(*refs):
    names = [*INPUTS, "out", *SCRATCH]
    m = SimpleNamespace(**dict(zip(names, refs, strict=True)))
    s = lax.axis_index("section")
    r = lax.axis_index("row")
    c = lax.axis_index("col")
    z, yh = r // 2, r % 2
    x, k = c // 2, c % 2
    quarter = 2 * yh + s
    sibling = (s, r, 2 * x + 1 - k)
    partner = (1 - s, 2 * z + 1 - yh, c)

    def ring_place(step):
        return (s, 2 * lax.rem(z + step + 8, 8) + yh, c)

    def col_place(step):
        return (s, r, lax.rem(c + step, 8))

    def plane_place(dy, ds, dx):
        return (lax.rem(s + ds, 2), 2 * z + lax.rem(yh + dy, 2), 2 * lax.rem(x + dx, 4) + k)

    def send(source, target, send_sem, recv_sem, place):
        copy = pltpu.make_async_remote_copy(
            src_ref=source,
            dst_ref=target,
            send_sem=send_sem,
            recv_sem=recv_sem,
            device_id=place,
            device_id_type=MESH,
        )
        copy.start()
        return copy

    sent = []

    def place(ds, dr, dc):
        return (
            lax.rem(s + ds, 2),
            lax.rem(r + dr + N_ROW, N_ROW),
            lax.rem(c + dc + N_COL, N_COL),
        )

    def load(source, target, index):
        copy = pltpu.make_async_copy(source, target, m.load_sem.at[index])
        copy.start()
        return copy

    own_cols = pl.ds(pl.multiple_of(quarter * BLOCK, BLOCK), BLOCK)
    other_cols = pl.ds(pl.multiple_of((3 - quarter) * BLOCK, BLOCK), BLOCK)
    load_expand = load(m.expand.at[:, own_cols], m.weights.at[z, 0, yh], 0)
    load_tokens = load(m.tokens, m.tokens_in, 1)
    load_factors = load(m.modulation, m.factors, 2)
    load_reduce = [
        load(m.reduce.at[:, own_cols], m.weights.at[z, 1, yh], 3),
    ]
    load_latent = load(m.latent_kernel, m.latent_in, 5)
    load_decode = load(m.decode_kernel, m.decode_in, 6)

    halo = []
    for ds in range(2):
        for dr in (-1, 0, 1):
            for dc in (-1, 0, 1):
                if (ds, dr, dc) != (0, 0, 0):
                    halo.append((ds, dr, dc))

    barrier = pltpu.get_barrier_semaphore()
    greet = [place(0, step, 0) for step in range(1, N_ROW)]
    greet += [col_place(step) for step in range(1, N_COL)]
    for dy, ds in ((0, 1), (1, 0), (1, 1)):
        greet += [plane_place(dy, ds, dx) for dx in range(4)]
    greet += [place(*h) for h in halo if h[0] * (h[1] or h[2]) or h[1] * h[2]]
    for target in greet:
        pl.semaphore_signal(barrier, inc=1, device_id=target, device_id_type=MESH)
    pl.semaphore_wait(barrier, len(greet))

    def to_partner(e, source):
        return send(
            source, m.weights.at[z, e, yh], m.partner_send.at[e], m.partner_recv.at[e], partner
        )

    from_partner = [to_partner(0, m.expand.at[:, other_cols])]
    ring = {}
    arrived = set()

    def ensure(e, o, way, d):
        if (e, o, way, d) not in arrived:
            ring[e, o, way, d].wait_recv()
            arrived.add((e, o, way, d))

    def reach(o, way):
        return 4 if (o == 0) == (way == 1) else 3

    def ring_step(e, d, units=(0, 1)):
        for o in units:
            half = lax.rem(yh + o, 2)
            for way in (1, -1):
                if d > reach(o, way):
                    continue
                if d > 1:
                    ensure(e, o, way, d - 1)
                held = m.weights.at[lax.rem(z - way * (d - 1) + 8, 8), e, half]
                index = (1 - way) // 2
                ring[e, o, way, d] = send(
                    held,
                    held,
                    m.ring_send.at[e, o, index, d - 1],
                    m.ring_recv.at[e, o, index, d - 1],
                    ring_place(way),
                )

    def arrive(e, d):
        for o in range(2):
            for way in (1, -1):
                if d <= reach(o, way):
                    ensure(e, o, way, d)

    load_expand.wait()
    ring_step(0, 1, (0,))

    load_tokens.wait()
    for slot in range(4):
        rows = m.tokens_in[m.order[slot]]
        for col in range(8):
            start = (slot // 2 * 4 + col // 2) * 16 + slot % 2 * 8
            m.tok[col % 2, start : start + 8, :] = jnp.concatenate(
                [rows[col * 4 : col * 4 + 4], rows[32 + col * 4 : 36 + col * 4]], axis=0
            )
    tok = m.tok[...].reshape(256, BLOCK)
    lane = lax.broadcasted_iota(jnp.int32, (256, 128), 1)
    token_sums = jnp.sum(tok, axis=1, keepdims=True)
    token_squares = jnp.sum(tok * tok, axis=1, keepdims=True)
    table = jnp.where(lane == 0, token_sums, jnp.where(lane == 1, token_squares, 0.0))
    m.stats[c] = table.T[:8]
    stat_copies = [
        send(m.stats.at[c], m.stats.at[c], m.stat_send.at[d], m.stat_recv.at[d], col_place(d))
        for d in range(1, 8)
    ]
    sent += stat_copies

    from_partner[0].wait_recv()
    ring_step(0, 1, (1,))

    load_factors.wait()
    lanes = pl.ds(pl.multiple_of(c * BLOCK, BLOCK), BLOCK)
    for slot in range(4):
        for j in range(3):
            m.first[j, slot // 2, slot % 2] = m.factors[j, pl.ds(m.order[slot], 1), lanes]

    for copy in stat_copies:
        copy.wait_recv()
    table = jnp.concatenate([jnp.sum(m.stats[...], axis=0), jnp.zeros((120, 256), F32)], axis=0).T
    token_mean = table[:, 0:1] * (1.0 / WIDTH)
    token_scale = lax.rsqrt(table[:, 1:2] * (1.0 / WIDTH) - token_mean * token_mean + EPSILON)
    plain = (tok - token_mean) * token_scale
    for core in range(2):
        for group in range(8):
            start = core * 128 + group * 16
            part = plain[start : start + 16].reshape(2, 8, BLOCK)
            part = part * (1.0 + m.first[1, group // 4]) + m.first[0, group // 4]
            m.normed[c, core, yh, pl.ds(group * 16, 16), :] = part.reshape(16, BLOCK).astype(BF16)

    mine = m.normed.at[c, :, yh]
    tok_copies = {}
    for dy, dx in ((1, 0), (0, 1), (0, 3), (1, 1), (1, 3), (0, 2), (1, 2)):
        tok_copies[dy, dx] = send(
            mine, mine, m.tok_send.at[dy, dx], m.tok_recv.at[dy, dx], plane_place(dy, dy, dx)
        )
    tok_copies[0, 0] = send(mine, mine, m.tok_send.at[0, 0], m.tok_recv.at[0, 0], sibling)
    sent += tok_copies.values()

    ring_step(0, 2)

    for copy in load_reduce:
        copy.wait()
    from_partner.append(to_partner(1, m.reduce.at[:, other_cols]))

    for core in range(2):
        for group in range(8):
            rows = pl.ds(group * 16, 16)
            part = m.tok[core, rows, :].reshape(2, 8, BLOCK)
            part = part + m.first[2, group // 4] * m.reduce_bias[...].reshape(1, BLOCK)
            m.based[core, rows, :] = part.reshape(16, BLOCK)
    base_copies = []
    for d in range(1, 8):
        target = lax.rem(c + d, 8)
        rows = pl.ds(pl.multiple_of((s * 4 + target // 2) * 16, 16), 16)
        base_copies.append(
            send(
                m.based.at[target % 2, rows, :],
                m.rows_in.at[c],
                m.base_send.at[d],
                m.base_recv.at[d],
                col_place(d),
            )
        )
    sent += base_copies
    own_rows = pl.ds(pl.multiple_of((s * 4 + x) * 16, 16), 16)
    m.rows_in[c] = m.based[k, own_rows, :]

    forwards = []

    def forward(dy, dx):
        tok_copies[dy, dx].wait_recv()
        piece = m.normed.at[2 * lax.rem(x - dx + 4, 4) + k, :, lax.rem(yh + dy, 2)]
        forwards.append(send(piece, piece, m.fwd_send.at[dy, dx], m.fwd_recv.at[dy, dx], sibling))

    forward(1, 0)
    ring_step(0, 3)
    for dy, dx in ((0, 1), (0, 3)):
        forward(dy, dx)

    source = lax.broadcasted_iota(jnp.int32, (64, 64), 0)
    target = lax.broadcasted_iota(jnp.int32, (64, 64), 1)
    swap = target == source % 4 * 16 + source // 4
    swap_bf16 = (source == target % 4 * 16 + target // 4).astype(F32).astype(BF16)
    patch_high = m.patch[...].astype(BF16)
    patch_low = (m.patch[...] - patch_high.astype(F32)).astype(BF16)
    m.patch_all[c] = jnp.concatenate(
        [jnp.dot(swap_bf16, part, preferred_element_type=F32) for part in (patch_high, patch_low)],
        axis=0,
    ).T.astype(BF16)
    patch_bias = jnp.dot(
        jnp.zeros((8, 64), F32) + m.patch_bias[...].reshape(1, 64),
        swap.astype(F32),
        preferred_element_type=F32,
        precision=lax.Precision.HIGHEST,
    )[:1]
    load_latent.wait()
    m.taps[...] = jnp.zeros_like(m.taps)
    for u in range(2):
        for v in range(2):
            for sa in range(2):
                for sb in range(2):
                    for a in range(2):
                        for b in range(2):
                            di = 2 * u + sa - 2 + a
                            dj = 2 * v + sb - 2 + b
                            if abs(di) <= 1 and abs(dj) <= 1:
                                row = ((u * 2 + v) * 2 + sa) * 2 + sb
                                tap = m.latent_in[di + 1, dj + 1]
                                high = tap.astype(jnp.bfloat16)
                                low = (tap - high.astype(jnp.float32)).astype(jnp.bfloat16)
                                phase = 2 * a + b
                                rows = pl.ds(row * 16, 16)
                                lanes = pl.ds(phase * 512, 512)
                                m.taps[0, rows, lanes] = high
                                m.taps[1, rows, lanes] = low
    m.patches[...] = jnp.zeros_like(m.patches)

    for slot in range(2):
        for j in range(3):
            for at in range(8):
                m.final[j, at, slot] = m.factors[
                    j + 2, pl.ds(m.order[2 * s + slot], 1), at * BLOCK : (at + 1) * BLOCK
                ]

    ring_step(1, 1, (0,))
    for dy, dx in ((1, 1), (1, 3)):
        forward(dy, dx)
    ring_step(0, 4)
    from_partner[1].wait_recv()
    ring_step(1, 1, (1,))
    for dy, dx in ((0, 2), (1, 2)):
        forward(dy, dx)
    sent += forwards

    patch_copies = [
        send(
            m.patch_all.at[c],
            m.patch_all.at[c],
            m.patch_send.at[d],
            m.patch_recv.at[d],
            col_place(d),
        )
        for d in range(1, 8)
    ]
    sent += patch_copies

    tok_copies[0, 0].wait_recv()
    for copy in forwards:
        copy.wait_recv()

    def expand(offset):
        at = lax.rem(z + offset + 8, 8)
        value = jnp.dot(
            m.normed[at].reshape(512, BLOCK),
            m.weights[at, 0].reshape(BLOCK, BLOCK),
            preferred_element_type=F32,
        )
        if offset == 0:
            m.total[...] = value
        else:
            m.total[...] += value

    arrive(0, 2)
    for offset in OFFSETS[:5]:
        expand(offset)
    ring_step(1, 2)
    arrive(0, 3)
    expand(-3)
    expand(3)
    arrive(0, 4)
    expand(4)
    value = m.total[...] + m.expand_bias[own_cols].reshape(1, BLOCK)
    inner = 0.7978845608028654 * (value + 0.044715 * (value * value * value))
    value = 0.5 * value * (1.0 + jnp.tanh(inner))
    m.hidden[...] = value.astype(BF16).reshape(2, 256, BLOCK)

    sib_copies = {}

    def contract(offset):
        slot = OFFSETS.index(offset)
        at = lax.rem(z + offset + 8, 8)
        right = m.weights[at, 1].reshape(BLOCK, BLOCK)
        away = lax.dot_general(
            m.hidden[1 - k], right, (((1,), (1,)), ((), ())), preferred_element_type=F32
        )
        m.sib_out[slot] = away.astype(BF16)
        sib_copies[slot] = send(
            m.sib_out.at[slot],
            m.sib_in.at[slot],
            m.sib_send.at[slot],
            m.sib_recv.at[slot],
            sibling,
        )
        m.kept[slot] = lax.dot_general(
            m.hidden[k], right, (((1,), (1,)), ((), ())), preferred_element_type=F32
        )

    m_own = yh * 8 + s * 4 + x
    sum_copies = {}

    def scatter(g):
        first_slot = OFFSETS.index(GROUPS[g][0])
        count = len(GROUPS[g])
        for slot in range(first_slot, first_slot + count):
            sib_copies[slot].wait_recv()
            value = m.kept[slot] + m.sib_in[slot].astype(F32)
            m.outgoing[slot] = value.astype(BF16).reshape(16, 16, BLOCK)
        slots = pl.ds(first_slot, count)
        for dx in (2, 1, 3, 0):
            for dy in range(2):
                for ds in range(2):
                    if (dy, ds, dx) == (0, 0, 0):
                        continue
                    there = plane_place(dy, ds, dx)
                    m_there = lax.rem(yh + dy, 2) * 8 + there[0] * 4 + lax.rem(x + dx, 4)
                    index = dy * 8 + ds * 4 + dx
                    sum_copies[g, index] = send(
                        m.outgoing.at[slots, m_there],
                        m.incoming.at[slots, m_own],
                        m.sum_send.at[g, index],
                        m.sum_recv.at[g, index],
                        there,
                    )
        m.incoming[slots, m_own] = m.outgoing[slots, m_own]

    contract(0)
    arrive(1, 1)
    contract(-1)
    contract(1)
    scatter(0)
    ring_step(1, 3)
    arrive(1, 2)
    contract(-2)
    contract(2)
    scatter(1)
    ring_step(1, 4)
    arrive(1, 3)
    contract(-3)
    contract(3)
    scatter(2)
    arrive(1, 4)
    contract(4)
    scatter(3)

    for copy in base_copies:
        copy.wait_recv()
    row_sums = jnp.zeros((2, 8, 1), F32)
    row_squares = jnp.zeros((2, 8, 1), F32)
    for g in range(4):
        for index in range(1, 16):
            sum_copies[g, index].wait_recv()
        for offset in GROUPS[g]:
            slot = OFFSETS.index(offset)
            at = lax.rem(z + offset + 8, 8)
            branch = jnp.sum(m.incoming[slot].astype(F32), axis=0).reshape(2, 8, BLOCK)
            value = m.rows_in[at].reshape(2, 8, BLOCK) + m.final[0, at] * branch
            m.residual[slot] = value
            row_sums += jnp.sum(value, axis=2, keepdims=True)
            row_squares += jnp.sum(value * value, axis=2, keepdims=True)
    row_mean = row_sums * (1.0 / WIDTH)
    row_scale = lax.rsqrt(row_squares * (1.0 / WIDTH) - row_mean * row_mean + EPSILON)
    for copy in patch_copies:
        copy.wait_recv()
    projected = jnp.zeros((32, 128), F32)
    for slot in range(8):
        at = lax.rem(z + OFFSETS[slot] + 8, 8)
        value = (m.residual[slot] - row_mean) * row_scale * (1.0 + m.final[2, at]) + m.final[1, at]
        value = value.reshape(16, BLOCK)
        high = value.astype(BF16)
        low = (value - high.astype(F32)).astype(BF16)
        projected += jnp.dot(
            jnp.concatenate([high, low], axis=0), m.patch_all[at], preferred_element_type=F32
        )
    patch = projected[:16, :64] + (projected[16:, :64] + projected[:16, 64:])
    latent = (patch + patch_bias) / 0.3611 + 0.1159
    latent = jnp.concatenate([latent, jnp.zeros((16, 64), F32)], axis=1)
    m.latents[...] = latent
    m.blocks[1, 1, s] = latent

    copies = []
    for ds, dr, dc in halo:
        copy = pltpu.make_async_remote_copy(
            src_ref=m.latents,
            dst_ref=m.blocks.at[1 - dr, 1 - dc, s],
            send_sem=m.halo_send.at[ds, 1 - dr, 1 - dc],
            recv_sem=m.halo_recv.at[ds, 1 - dr, 1 - dc],
            device_id=place(ds, dr, dc),
            device_id_type=MESH,
        )
        copy.start()
        copies.append(copy)

    for copy in copies:
        copy.wait()

    for ds in range(2):
        for dr in (-1, 0, 1):
            for dc in (-1, 0, 1):
                inside = (r + dr >= 0) & (r + dr < N_ROW) & (c + dc >= 0) & (c + dc < N_COL)
                keep = jnp.where(inside, 1.0, 0.0).astype(jnp.float32)
                block = m.blocks[dr + 1, dc + 1, ds][:, :64] * keep
                rows = {-1: ((1, 0),), 0: ((0, 1), (1, 2)), 1: ((0, 3),)}[dr]
                first, count, at = {-1: (3, 1, 0), 0: (0, 4, 1), 1: (0, 1, 5)}[dc]
                for mb in range(2):
                    for source, target in rows:
                        start = mb * 8 + source * 4 + first
                        m.patches[2 * ds + mb, target, at : at + count, :] = block[
                            start : start + count
                        ]

    slabs = [
        m.patches[:, u : u + 3, v : v + 8, :].reshape(96, 64) for u in range(2) for v in range(2)
    ]
    window = jnp.concatenate(slabs, axis=-1)
    high = window.astype(jnp.bfloat16)
    low = (window - high.astype(jnp.float32)).astype(jnp.bfloat16)
    both = jnp.concatenate([high, low], axis=0)

    jj = lax.broadcasted_iota(jnp.int32, (96, 1), 0) % 8
    ii = (lax.broadcasted_iota(jnp.int32, (96, 1), 0) // 8) % 3
    sums = jnp.zeros((4, 512), jnp.float32)
    squares = jnp.zeros((4, 512), jnp.float32)
    for a in range(2):
        for b in range(2):
            phase = 2 * a + b
            lanes = pl.ds(phase * 512, 512)
            first = jnp.dot(both, m.taps[0, :, lanes], preferred_element_type=jnp.float32)
            second = jnp.dot(high, m.taps[1, :, lanes], preferred_element_type=jnp.float32)
            value = first[:96] + (first[96:] + second) + m.latent_bias[...]
            m.act[phase] = value
            own = (ii >= a) & (ii < a + 2) & (jj >= b) & (jj < b + 4)
            masked = jnp.where(own, value, 0.0).reshape(4, 24, 512)
            sums += jnp.sum(masked, axis=1)
            squares += jnp.sum(masked * masked, axis=1)

    chan = lax.broadcasted_iota(jnp.int32, (512, 128), 0) // 16
    member = (chan == lax.broadcasted_iota(jnp.int32, (512, 128), 1)).astype(jnp.float32)
    chan_t = lax.broadcasted_iota(jnp.int32, (128, 512), 1) // 16
    member_t = (chan_t == lax.broadcasted_iota(jnp.int32, (128, 512), 0)).astype(jnp.float32)
    stats = jnp.dot(
        jnp.concatenate([sums, squares], axis=0),
        member,
        preferred_element_type=jnp.float32,
        precision=lax.Precision.HIGHEST,
    )

    m.col_stats[c] = stats
    copies = []
    for dc in range(1, N_COL):
        copy = pltpu.make_async_remote_copy(
            src_ref=m.col_stats.at[c],
            dst_ref=m.col_stats.at[c],
            send_sem=m.col_send.at[dc],
            recv_sem=m.col_recv.at[dc],
            device_id=place(0, 0, dc),
            device_id_type=MESH,
        )
        copy.start()
        copies.append(copy)
    for copy in copies:
        copy.wait()
    m.row_stats[r] = jnp.sum(m.col_stats[...], axis=0)
    copies = []
    for dr in range(1, N_ROW):
        copy = pltpu.make_async_remote_copy(
            src_ref=m.row_stats.at[r],
            dst_ref=m.row_stats.at[r],
            send_sem=m.row_send.at[dr],
            recv_sem=m.row_recv.at[dr],
            device_id=place(0, dr, 0),
            device_id_type=MESH,
        )
        copy.start()
        copies.append(copy)
    for copy in copies:
        copy.wait()
    total = jnp.sum(m.row_stats[...], axis=0) * (1.0 / CELLS)
    mean = total[:4]
    scale = lax.rsqrt(total[4:] - mean * mean + EPSILON)
    spread = jnp.dot(
        jnp.concatenate([mean, scale], axis=0),
        member_t,
        preferred_element_type=jnp.float32,
        precision=lax.Precision.HIGHEST,
    )

    for a in range(2):
        for b in range(2):
            phase = 2 * a + b
            line = 4 * r + 2 * ii - a
            across = 8 * c + 2 * jj - b
            inside = (line >= 0) & (line < 64) & (across >= 0) & (across < 64)
            parts = []
            for mb in range(4):
                value = m.act[phase, mb * 24 : mb * 24 + 24]
                value = (value - spread[mb : mb + 1]) * (
                    spread[4 + mb : 5 + mb] * m.gain[...]
                ) + m.shift[...]
                parts.append(value / (1.0 + jnp.exp(-value)))
            value = jnp.where(inside, jnp.concatenate(parts, axis=0), 0.0)
            m.cells[phase * 96 : phase * 96 + 96, :] = value.astype(jnp.bfloat16)

    load_decode.wait()
    for tap in range(9):
        value = jnp.dot(m.cells[...], m.decode_in[tap], preferred_element_type=jnp.float32)
        m.products[tap] = value.reshape(4, 4, 3, 8, 256)

    for a in range(2):
        for b in range(2):
            for up in range(2):
                for left in range(2):
                    total = jnp.zeros((4, 2, 4, 256), jnp.float32) + m.decode_bias[...]
                    for di in range(3):
                        row_phase, row_at = phase_of(a, (up + di - 1) // 2)
                        for dj in range(3):
                            col_phase, col_at = phase_of(b, (left + dj - 1) // 2)
                            total += m.products[
                                di * 3 + dj,
                                row_phase * 2 + col_phase,
                                :,
                                row_at : row_at + 2,
                                col_at : col_at + 4,
                                :,
                            ]
                    for mb in range(4):
                        for i in range(2):
                            for half in range(2):
                                m.out[
                                    half,
                                    mb,
                                    4 * i + 2 * a + up,
                                    pl.ds(2 * b + left, 4, stride=4),
                                    :,
                                ] = total[mb, i, :, half * 128 : half * 128 + 128]

    for copy in from_partner:
        copy.wait_send()
    for copy in ring.values():
        copy.wait_send()
    for copy in sent:
        copy.wait_send()
    for copy in sib_copies.values():
        copy.wait_send()
    for copy in sum_copies.values():
        copy.wait_send()


def shards(*args):
    shapes = {
        "latent_bias": (1, 512),
        "gain": (1, 512),
        "shift": (1, 512),
        "decode_kernel": (9, 512, 256),
        "decode_bias": (1, 256),
    }
    turned = {"modulation": (1, 0, 2), "reduce": (1, 0), "patch": (1, 0)}
    args = [
        a.transpose(turned[name]) if name in turned else a.reshape(shapes.get(name, a.shape))
        for name, a in zip(INPUTS, args, strict=True)
    ]
    out = pl.pallas_call(
        program_kernel,
        out_shape=jax.ShapeDtypeStruct((2, 4, 8, 16, 128), F32),
        in_specs=[pl.BlockSpec(memory_space=space) for space in INPUTS.values()],
        out_specs=pl.BlockSpec(memory_space=pltpu.VMEM),
        scratch_shapes=list(SCRATCH.values()),
        compiler_params=pltpu.CompilerParams(
            collective_id=0, has_side_effects=True, vmem_limit_bytes=56 * 2**20
        ),
    )(*args)
    return out.transpose(1, 2, 3, 0, 4).reshape(4, 8, 16, 256)


def solution(mesh):
    return jax.shard_map(
        shards,
        mesh=mesh,
        in_specs=(
            P(None, "row", "col"),
            P(),
            P(),
            P("row", "col"),
            P("col"),
            P("col", "row"),
            P("col"),
            P("col", None),
            P(),
            P(),
            P(),
            P(),
            P(),
            P(None, None, None, "section"),
            P("section"),
        ),
        out_specs=P(None, "row", "col", "section"),
        check_vma=False,
    )
```

```python
from types import SimpleNamespace

import jax
import jax.numpy as jnp
from jax import lax
from jax.experimental import pallas as pl
from jax.experimental.pallas import tpu as pltpu
from jax.sharding import PartitionSpec as P

MESH = pl.DeviceIdType.MESH
EPSILON = 1e-06
N_ROW = 16
N_COL = 8
CELLS = 64 * 64 * 16
WIDTH = 3072
BLOCK = 384
PIECE = 192
GROUPS = ((0, -1, 1), (-2, 2), (-3, 3), (4,))
OFFSETS = (0, -1, 1, -2, 2, -3, 3, 4)
BF16, F32 = jnp.bfloat16, jnp.float32
DMA = pltpu.SemaphoreType.DMA
INPUTS = {
    "tokens": pl.ANY,
    "order": pltpu.SMEM,
    "modulation": pl.ANY,
    "expand": pl.ANY,
    "expand_bias": pltpu.VMEM,
    "reduce": pl.ANY,
    "reduce_bias": pltpu.VMEM,
    "patch": pltpu.VMEM,
    "patch_bias": pltpu.VMEM,
    "latent_kernel": pl.ANY,
    "latent_bias": pltpu.VMEM,
    "gain": pltpu.VMEM,
    "shift": pltpu.VMEM,
    "decode_kernel": pl.ANY,
    "decode_bias": pltpu.VMEM,
}
SCRATCH = {
    "tokens_in": pltpu.VMEM((4, 64, BLOCK), F32),
    "factors": pltpu.VMEM((5, 4, WIDTH), F32),
    "latent_in": pltpu.VMEM((3, 3, 16, 512), F32),
    "decode_in": pltpu.VMEM((9, 512, 256), BF16),
    "tok": pltpu.VMEM((2, 128, BLOCK), F32),
    "first": pltpu.VMEM((3, 2, 2, 1, BLOCK), F32),
    "final": pltpu.VMEM((3, 8, 2, 1, BLOCK), F32),
    "normed": pltpu.VMEM((8, 2, 2, 128, BLOCK), BF16),
    "weights": pltpu.VMEM((8, 2, 2, PIECE, BLOCK), BF16),
    "total": pltpu.VMEM((512, BLOCK), F32),
    "hidden": pltpu.VMEM((2, 256, BLOCK), BF16),
    "based": pltpu.VMEM((2, 128, BLOCK), F32),
    "rows_in": pltpu.VMEM((8, 16, BLOCK), F32),
    "patch_all": pltpu.VMEM((8, BLOCK, 128), BF16),
    "stats": pltpu.VMEM((8, 8, 256), F32),
    "sib_out": pltpu.VMEM((8, 256, BLOCK), BF16),
    "sib_in": pltpu.VMEM((8, 256, BLOCK), BF16),
    "kept": pltpu.VMEM((8, 256, BLOCK), F32),
    "outgoing": pltpu.VMEM((8, 16, 16, BLOCK), BF16),
    "incoming": pltpu.VMEM((8, 16, 16, BLOCK), BF16),
    "residual": pltpu.VMEM((8, 2, 8, BLOCK), F32),
    "latents": pltpu.VMEM((16, 128), F32),
    "blocks": pltpu.VMEM((3, 3, 2, 16, 128), F32),
    "patches": pltpu.VMEM((4, 4, 16, 64), F32),
    "taps": pltpu.VMEM((2, 256, 2048), BF16),
    "act": pltpu.VMEM((4, 96, 512), F32),
    "cells": pltpu.VMEM((384, 512), BF16),
    "products": pltpu.VMEM((9, 4, 4, 3, 8, 256), F32),
    "col_stats": pltpu.VMEM((8, 8, 128), F32),
    "row_stats": pltpu.VMEM((16, 8, 128), F32),
    "staged": pltpu.VMEM((2, 4, 8, 16, 128), F32),
    "member": pltpu.VMEM((512, 128), F32),
    "member_t": pltpu.VMEM((128, 512), F32),
    "load_sem": DMA((8,)),
    "partner_send": DMA((2,)),
    "partner_recv": DMA((2,)),
    "ring_send": DMA((2, 2, 2, 4)),
    "ring_recv": DMA((2, 2, 2, 4)),
    "stat_send": DMA((8,)),
    "stat_recv": DMA((8,)),
    "base_send": DMA((8,)),
    "base_recv": DMA((8,)),
    "patch_send": DMA((2, 4)),
    "patch_recv": DMA((2, 4)),
    "tok_send": DMA((2, 4)),
    "tok_recv": DMA((2, 4)),
    "fwd_send": DMA((2, 4)),
    "fwd_recv": DMA((2, 4)),
    "sib_send": DMA((8,)),
    "sib_recv": DMA((8,)),
    "sum_send": DMA((4, 16)),
    "sum_recv": DMA((4, 16)),
    "halo_send": DMA((2, 3, 3)),
    "halo_recv": DMA((2, 3, 3)),
    "col_send": DMA((8,)),
    "col_recv": DMA((8,)),
    "row_send": DMA((16,)),
    "row_recv": DMA((16,)),
}


def phase_of(base, step):
    if base == 0:
        return [(1, 0), (0, 0), (1, 1)][step + 1]
    return [(0, 0), (1, 1), (0, 1)][step + 1]


def program_kernel(*refs):
    names = [*INPUTS, "out", *SCRATCH]
    m = SimpleNamespace(**dict(zip(names, refs, strict=True)))
    s = lax.axis_index("section")
    r = lax.axis_index("row")
    c = lax.axis_index("col")
    z, yh = r // 2, r % 2
    x, k = c // 2, c % 2
    quarter = 2 * yh + s
    sibling = (s, r, 2 * x + 1 - k)
    partner = (1 - s, 2 * z + 1 - yh, c)

    def ring_place(step):
        return (s, 2 * lax.rem(z + step + 8, 8) + yh, c)

    def col_place(step):
        return (s, r, lax.rem(c + step, 8))

    def plane_place(dy, ds, dx):
        return (lax.rem(s + ds, 2), 2 * z + lax.rem(yh + dy, 2), 2 * lax.rem(x + dx, 4) + k)

    def send(source, target, send_sem, recv_sem, place):
        copy = pltpu.make_async_remote_copy(
            src_ref=source,
            dst_ref=target,
            send_sem=send_sem,
            recv_sem=recv_sem,
            device_id=place,
            device_id_type=MESH,
        )
        copy.start()
        return copy

    sent = []

    def place(ds, dr, dc):
        return (
            lax.rem(s + ds, 2),
            lax.rem(r + dr + N_ROW, N_ROW),
            lax.rem(c + dc + N_COL, N_COL),
        )

    def load(source, target, index):
        copy = pltpu.make_async_copy(source, target, m.load_sem.at[index])
        copy.start()
        return copy

    own_cols = pl.ds(pl.multiple_of(quarter * BLOCK, BLOCK), BLOCK)
    other_cols = pl.ds(pl.multiple_of((3 - quarter) * BLOCK, BLOCK), BLOCK)
    load_expand = load(m.expand.at[:, own_cols], m.weights.at[z, 0, yh], 0)
    load_tokens = load(m.tokens, m.tokens_in, 1)
    load_factors = load(m.modulation, m.factors, 2)
    load_reduce = [
        load(m.reduce.at[:, own_cols], m.weights.at[z, 1, yh], 3),
    ]
    load_latent = load(m.latent_kernel, m.latent_in, 5)
    load_decode = load(m.decode_kernel, m.decode_in, 6)

    halo = []
    for ds in range(2):
        for dr in (-1, 0, 1):
            for dc in (-1, 0, 1):
                if (ds, dr, dc) != (0, 0, 0):
                    halo.append((ds, dr, dc))

    barrier = pltpu.get_barrier_semaphore()
    greet = [place(0, step, 0) for step in range(1, N_ROW)]
    greet += [col_place(step) for step in range(1, N_COL)]
    for dy, ds in ((0, 1), (1, 0), (1, 1)):
        greet += [plane_place(dy, ds, dx) for dx in range(4)]
    greet += [place(*h) for h in halo if h[0] * (h[1] or h[2]) or h[1] * h[2]]
    for target in greet:
        pl.semaphore_signal(barrier, inc=1, device_id=target, device_id_type=MESH)
    pl.semaphore_wait(barrier, len(greet))

    def to_partner(e, source):
        return send(
            source, m.weights.at[z, e, yh], m.partner_send.at[e], m.partner_recv.at[e], partner
        )

    from_partner = [to_partner(0, m.expand.at[:, other_cols])]
    ring = {}
    arrived = set()

    def ensure(e, o, way, d):
        if (e, o, way, d) not in arrived:
            ring[e, o, way, d].wait_recv()
            arrived.add((e, o, way, d))

    def reach(o, way):
        return 4 if (o == 0) == (way == 1) else 3

    def ring_step(e, d, units=(0, 1)):
        for o in units:
            half = lax.rem(yh + o, 2)
            for way in (1, -1):
                if d > reach(o, way):
                    continue
                if d > 1:
                    ensure(e, o, way, d - 1)
                held = m.weights.at[lax.rem(z - way * (d - 1) + 8, 8), e, half]
                index = (1 - way) // 2
                ring[e, o, way, d] = send(
                    held,
                    held,
                    m.ring_send.at[e, o, index, d - 1],
                    m.ring_recv.at[e, o, index, d - 1],
                    ring_place(way),
                )

    def arrive(e, d):
        for o in range(2):
            for way in (1, -1):
                if d <= reach(o, way):
                    ensure(e, o, way, d)

    load_expand.wait()
    ring_step(0, 1, (0,))

    load_tokens.wait()
    for slot in range(4):
        rows = m.tokens_in[m.order[slot]]
        for col in range(8):
            start = (slot // 2 * 4 + col // 2) * 16 + slot % 2 * 8
            m.tok[col % 2, start : start + 8, :] = jnp.concatenate(
                [rows[col * 4 : col * 4 + 4], rows[32 + col * 4 : 36 + col * 4]], axis=0
            )
    tok = m.tok[...].reshape(256, BLOCK)
    lane = lax.broadcasted_iota(jnp.int32, (256, 128), 1)
    token_sums = jnp.sum(tok, axis=1, keepdims=True)
    token_squares = jnp.sum(tok * tok, axis=1, keepdims=True)
    table = jnp.where(lane == 0, token_sums, jnp.where(lane == 1, token_squares, 0.0))
    m.stats[c] = table.T[:8]
    stat_copies = [
        send(m.stats.at[c], m.stats.at[c], m.stat_send.at[d], m.stat_recv.at[d], col_place(d))
        for d in range(1, 8)
    ]
    sent += stat_copies

    from_partner[0].wait_recv()
    ring_step(0, 1, (1,))

    load_factors.wait()
    lanes = pl.ds(pl.multiple_of(c * BLOCK, BLOCK), BLOCK)
    for slot in range(4):
        for j in range(3):
            m.first[j, slot // 2, slot % 2] = m.factors[j, pl.ds(m.order[slot], 1), lanes]

    source = lax.broadcasted_iota(jnp.int32, (64, 64), 0)
    target = lax.broadcasted_iota(jnp.int32, (64, 64), 1)
    swap = target == source % 4 * 16 + source // 4
    swap_bf16 = (source == target % 4 * 16 + target // 4).astype(F32).astype(BF16)
    patch_high = m.patch[...].astype(BF16)
    patch_low = (m.patch[...] - patch_high.astype(F32)).astype(BF16)
    m.patch_all[c] = jnp.concatenate(
        [jnp.dot(swap_bf16, part, preferred_element_type=F32) for part in (patch_high, patch_low)],
        axis=0,
    ).T.astype(BF16)
    patch_bias = jnp.dot(
        jnp.zeros((8, 64), F32) + m.patch_bias[...].reshape(1, 64),
        swap.astype(F32),
        preferred_element_type=F32,
        precision=lax.Precision.HIGHEST,
    )[:1]
    load_latent.wait()
    m.taps[...] = jnp.zeros_like(m.taps)
    for u in range(2):
        for v in range(2):
            for sa in range(2):
                for sb in range(2):
                    for a in range(2):
                        for b in range(2):
                            di = 2 * u + sa - 2 + a
                            dj = 2 * v + sb - 2 + b
                            if abs(di) <= 1 and abs(dj) <= 1:
                                row = ((u * 2 + v) * 2 + sa) * 2 + sb
                                tap = m.latent_in[di + 1, dj + 1]
                                high = tap.astype(jnp.bfloat16)
                                low = (tap - high.astype(jnp.float32)).astype(jnp.bfloat16)
                                phase = 2 * a + b
                                rows = pl.ds(row * 16, 16)
                                lanes = pl.ds(phase * 512, 512)
                                m.taps[0, rows, lanes] = high
                                m.taps[1, rows, lanes] = low
    m.patches[...] = jnp.zeros_like(m.patches)
    chan = lax.broadcasted_iota(jnp.int32, (512, 128), 0) // 16
    m.member[...] = (chan == lax.broadcasted_iota(jnp.int32, (512, 128), 1)).astype(jnp.float32)
    chan_t = lax.broadcasted_iota(jnp.int32, (128, 512), 1) // 16
    m.member_t[...] = (chan_t == lax.broadcasted_iota(jnp.int32, (128, 512), 0)).astype(jnp.float32)

    for slot in range(2):
        for j in range(3):
            for at in range(8):
                m.final[j, at, slot] = m.factors[
                    j + 2, pl.ds(m.order[2 * s + slot], 1), at * BLOCK : (at + 1) * BLOCK
                ]

    for copy in stat_copies:
        copy.wait_recv()
    ring_step(0, 2, (0,))
    table = jnp.concatenate([jnp.sum(m.stats[...], axis=0), jnp.zeros((120, 256), F32)], axis=0).T
    token_mean = table[:, 0:1] * (1.0 / WIDTH)
    token_scale = lax.rsqrt(table[:, 1:2] * (1.0 / WIDTH) - token_mean * token_mean + EPSILON)
    plain = (tok - token_mean) * token_scale
    for core in range(2):
        for group in range(8):
            start = core * 128 + group * 16
            part = plain[start : start + 16].reshape(2, 8, BLOCK)
            part = part * (1.0 + m.first[1, group // 4]) + m.first[0, group // 4]
            m.normed[c, core, yh, pl.ds(group * 16, 16), :] = part.reshape(16, BLOCK).astype(BF16)

    tok_copies = {}

    def share(dy, dx, col, half, target):
        piece = m.normed.at[col, :, half]
        tok_copies[dy, dx] = send(
            piece, piece, m.tok_send.at[dy, dx], m.tok_recv.at[dy, dx], target
        )

    share(1, 0, c, yh, partner)
    for dx in (3, 1, 2):
        share(0, dx, c, yh, plane_place(0, 0, dx))
    share(0, 0, c, yh, sibling)

    ring_step(0, 2, (1,))

    for copy in load_reduce:
        copy.wait()
    from_partner.append(to_partner(1, m.reduce.at[:, other_cols]))

    for core in range(2):
        for group in range(8):
            rows = pl.ds(group * 16, 16)
            part = m.tok[core, rows, :].reshape(2, 8, BLOCK)
            part = part + m.first[2, group // 4] * m.reduce_bias[...].reshape(1, BLOCK)
            m.based[core, rows, :] = part.reshape(16, BLOCK)
    base_copies = []
    for d in range(1, 8):
        target = lax.rem(c + d, 8)
        rows = pl.ds(pl.multiple_of((s * 4 + target // 2) * 16, 16), 16)
        base_copies.append(
            send(
                m.based.at[target % 2, rows, :],
                m.rows_in.at[c],
                m.base_send.at[d],
                m.base_recv.at[d],
                col_place(d),
            )
        )
    sent += base_copies
    own_rows = pl.ds(pl.multiple_of((s * 4 + x) * 16, 16), 16)
    m.rows_in[c] = m.based[k, own_rows, :]

    forwards = []

    def forward(dy, dx):
        tok_copies[dy, dx].wait_recv()
        col, half = 2 * lax.rem(x - dx + 4, 4) + k, lax.rem(yh + dy, 2)
        if (dy, dx) == (1, 0):
            share(1, 1, col, half, plane_place(0, 0, 1))
        if dy == 0 and dx > 1:
            share(1, dx, col, half, partner)
        piece = m.normed.at[col, :, half]
        forwards.append(send(piece, piece, m.fwd_send.at[dy, dx], m.fwd_recv.at[dy, dx], sibling))

    for dy, dx in ((1, 0), (0, 3), (0, 1)):
        forward(dy, dx)
    ring_step(0, 3)
    for dy, dx in ((0, 2), (1, 1), (1, 3)):
        forward(dy, dx)
    ring_step(0, 4)
    from_partner[1].wait_recv()
    ring_step(1, 1)
    forward(1, 2)
    sent += forwards
    sent += tok_copies.values()

    patch_copies = [
        send(
            m.patch_all.at[c],
            m.patch_all.at[c],
            m.patch_send.at[0, d],
            m.patch_recv.at[0, d],
            plane_place(0, 0, d) if d else sibling,
        )
        for d in (1, 3, 2, 0)
    ]
    sent += patch_copies

    tok_copies[0, 0].wait_recv()
    for copy in forwards:
        copy.wait_recv()

    def expand(offset):
        at = lax.rem(z + offset + 8, 8)
        value = jnp.dot(
            m.normed[at].reshape(512, BLOCK),
            m.weights[at, 0].reshape(BLOCK, BLOCK),
            preferred_element_type=F32,
        )
        if offset == 0:
            m.total[...] = value
        else:
            m.total[...] += value

    arrive(0, 2)
    for offset in OFFSETS[:5]:
        expand(offset)
    arrive(0, 3)
    expand(-3)
    expand(3)
    arrive(0, 4)
    expand(4)
    value = m.total[...] + m.expand_bias[own_cols].reshape(1, BLOCK)
    inner = 0.7978845608028654 * (value + 0.044715 * (value * value * value))
    value = 0.5 * value * (1.0 + jnp.tanh(inner))
    m.hidden[...] = value.astype(BF16).reshape(2, 256, BLOCK)

    sib_copies = {}

    def contract(offset):
        slot = OFFSETS.index(offset)
        at = lax.rem(z + offset + 8, 8)
        right = m.weights[at, 1].reshape(BLOCK, BLOCK)
        away = lax.dot_general(
            m.hidden[1 - k], right, (((1,), (1,)), ((), ())), preferred_element_type=F32
        )
        m.sib_out[slot] = away.astype(BF16)
        sib_copies[slot] = send(
            m.sib_out.at[slot],
            m.sib_in.at[slot],
            m.sib_send.at[slot],
            m.sib_recv.at[slot],
            sibling,
        )
        m.kept[slot] = lax.dot_general(
            m.hidden[k], right, (((1,), (1,)), ((), ())), preferred_element_type=F32
        )

    m_own = yh * 8 + s * 4 + x
    sum_copies = {}

    def scatter(g):
        first_slot = OFFSETS.index(GROUPS[g][0])
        count = len(GROUPS[g])
        for slot in range(first_slot, first_slot + count):
            sib_copies[slot].wait_recv()
            value = m.kept[slot] + m.sib_in[slot].astype(F32)
            m.outgoing[slot] = value.astype(BF16).reshape(16, 16, BLOCK)
        slots = pl.ds(first_slot, count)
        for dx in (2, 1, 3, 0):
            for dy in range(2):
                for ds in range(2):
                    if (dy, ds, dx) == (0, 0, 0):
                        continue
                    there = plane_place(dy, ds, dx)
                    m_there = lax.rem(yh + dy, 2) * 8 + there[0] * 4 + lax.rem(x + dx, 4)
                    index = dy * 8 + ds * 4 + dx
                    sum_copies[g, index] = send(
                        m.outgoing.at[slots, m_there],
                        m.incoming.at[slots, m_own],
                        m.sum_send.at[g, index],
                        m.sum_recv.at[g, index],
                        there,
                    )
        m.incoming[slots, m_own] = m.outgoing[slots, m_own]

    row_parts = []

    def collect(g):
        for index in range(1, 16):
            sum_copies[g, index].wait_recv()
        for offset in GROUPS[g]:
            slot = OFFSETS.index(offset)
            at = lax.rem(z + offset + 8, 8)
            branch = jnp.sum(m.incoming[slot].astype(F32), axis=0).reshape(2, 8, BLOCK)
            value = m.rows_in[at].reshape(2, 8, BLOCK) + m.final[0, at] * branch
            m.residual[slot] = value
            row_parts.append(
                (
                    jnp.sum(value, axis=2, keepdims=True),
                    jnp.sum(value * value, axis=2, keepdims=True),
                )
            )

    patch_forwards = []
    for d, copy in zip((1, 3, 2), patch_copies):
        copy.wait_recv()
        piece = m.patch_all.at[2 * lax.rem(x - d + 4, 4) + k]
        patch_forwards.append(
            send(piece, piece, m.patch_send.at[1, d], m.patch_recv.at[1, d], sibling)
        )
    sent += patch_forwards

    contract(0)
    ring_step(1, 2)
    arrive(1, 1)
    contract(-1)
    contract(1)
    scatter(0)
    ring_step(1, 3)
    arrive(1, 2)
    contract(-2)
    contract(2)
    scatter(1)
    ring_step(1, 4)
    for copy in base_copies:
        copy.wait_recv()
    arrive(1, 3)
    contract(-3)
    contract(3)
    scatter(2)
    collect(0)
    arrive(1, 4)
    contract(4)
    scatter(3)
    for g in range(1, 4):
        collect(g)
    row_sums = sum(part[0] for part in row_parts)
    row_squares = sum(part[1] for part in row_parts)
    row_mean = row_sums * (1.0 / WIDTH)
    row_scale = lax.rsqrt(row_squares * (1.0 / WIDTH) - row_mean * row_mean + EPSILON)
    for copy in (patch_copies[3], *patch_forwards):
        copy.wait_recv()
    projected = jnp.zeros((32, 128), F32)
    for slot in range(8):
        at = lax.rem(z + OFFSETS[slot] + 8, 8)
        value = (m.residual[slot] - row_mean) * row_scale * (1.0 + m.final[2, at]) + m.final[1, at]
        value = value.reshape(16, BLOCK)
        high = value.astype(BF16)
        low = (value - high.astype(F32)).astype(BF16)
        projected += jnp.dot(
            jnp.concatenate([high, low], axis=0), m.patch_all[at], preferred_element_type=F32
        )
    patch = projected[:16, :64] + (projected[16:, :64] + projected[:16, 64:])
    latent = (patch + patch_bias) / 0.3611 + 0.1159
    latent = jnp.concatenate([latent, jnp.zeros((16, 64), F32)], axis=1)
    m.latents[...] = latent
    m.blocks[1, 1, s] = latent

    copies = []
    for ds, dr, dc in halo:
        copy = pltpu.make_async_remote_copy(
            src_ref=m.latents,
            dst_ref=m.blocks.at[1 - dr, 1 - dc, s],
            send_sem=m.halo_send.at[ds, 1 - dr, 1 - dc],
            recv_sem=m.halo_recv.at[ds, 1 - dr, 1 - dc],
            device_id=place(ds, dr, dc),
            device_id_type=MESH,
        )
        copy.start()
        copies.append(copy)

    for copy in copies:
        copy.wait_recv()
    sent += copies

    for ds in range(2):
        for dr in (-1, 0, 1):
            for dc in (-1, 0, 1):
                inside = (r + dr >= 0) & (r + dr < N_ROW) & (c + dc >= 0) & (c + dc < N_COL)
                keep = jnp.where(inside, 1.0, 0.0).astype(jnp.float32)
                block = m.blocks[dr + 1, dc + 1, ds][:, :64] * keep
                rows = {-1: ((1, 0),), 0: ((0, 1), (1, 2)), 1: ((0, 3),)}[dr]
                first, count, at = {-1: (3, 1, 0), 0: (0, 4, 1), 1: (0, 1, 5)}[dc]
                for mb in range(2):
                    for source, target in rows:
                        start = mb * 8 + source * 4 + first
                        m.patches[2 * ds + mb, target, at : at + count, :] = block[
                            start : start + count
                        ]

    slabs = [
        m.patches[:, u : u + 3, v : v + 8, :].reshape(96, 64) for u in range(2) for v in range(2)
    ]
    window = jnp.concatenate(slabs, axis=-1)
    high = window.astype(jnp.bfloat16)
    low = (window - high.astype(jnp.float32)).astype(jnp.bfloat16)
    both = jnp.concatenate([high, low], axis=0)

    jj = lax.broadcasted_iota(jnp.int32, (96, 1), 0) % 8
    ii = (lax.broadcasted_iota(jnp.int32, (96, 1), 0) // 8) % 3
    sums = jnp.zeros((4, 512), jnp.float32)
    squares = jnp.zeros((4, 512), jnp.float32)
    for a in range(2):
        for b in range(2):
            phase = 2 * a + b
            lanes = pl.ds(phase * 512, 512)
            first = jnp.dot(both, m.taps[0, :, lanes], preferred_element_type=jnp.float32)
            second = jnp.dot(high, m.taps[1, :, lanes], preferred_element_type=jnp.float32)
            value = first[:96] + (first[96:] + second) + m.latent_bias[...]
            m.act[phase] = value
            own = (ii >= a) & (ii < a + 2) & (jj >= b) & (jj < b + 4)
            masked = jnp.where(own, value, 0.0).reshape(4, 24, 512)
            sums += jnp.sum(masked, axis=1)
            squares += jnp.sum(masked * masked, axis=1)

    stats = jnp.dot(
        jnp.concatenate([sums, squares], axis=0),
        m.member[...],
        preferred_element_type=jnp.float32,
        precision=lax.Precision.HIGHEST,
    )

    m.col_stats[c] = stats
    copies = []
    for dc in range(1, N_COL):
        copy = pltpu.make_async_remote_copy(
            src_ref=m.col_stats.at[c],
            dst_ref=m.col_stats.at[c],
            send_sem=m.col_send.at[dc],
            recv_sem=m.col_recv.at[dc],
            device_id=place(0, 0, dc),
            device_id_type=MESH,
        )
        copy.start()
        copies.append(copy)
    for copy in copies:
        copy.wait_recv()
    sent += copies
    m.row_stats[r] = jnp.sum(m.col_stats[...], axis=0)
    copies = []
    for dr in range(1, N_ROW):
        copy = pltpu.make_async_remote_copy(
            src_ref=m.row_stats.at[r],
            dst_ref=m.row_stats.at[r],
            send_sem=m.row_send.at[dr],
            recv_sem=m.row_recv.at[dr],
            device_id=place(0, dr, 0),
            device_id_type=MESH,
        )
        copy.start()
        copies.append(copy)
    for copy in copies:
        copy.wait_recv()
    sent += copies
    total = jnp.sum(m.row_stats[...], axis=0) * (1.0 / CELLS)
    mean = total[:4]
    scale = lax.rsqrt(total[4:] - mean * mean + EPSILON)
    spread = jnp.dot(
        jnp.concatenate([mean, scale], axis=0),
        m.member_t[...],
        preferred_element_type=jnp.float32,
        precision=lax.Precision.HIGHEST,
    )

    for a in range(2):
        for b in range(2):
            phase = 2 * a + b
            line = 4 * r + 2 * ii - a
            across = 8 * c + 2 * jj - b
            inside = (line >= 0) & (line < 64) & (across >= 0) & (across < 64)
            parts = []
            for mb in range(4):
                value = m.act[phase, mb * 24 : mb * 24 + 24]
                value = (value - spread[mb : mb + 1]) * (
                    spread[4 + mb : 5 + mb] * m.gain[...]
                ) + m.shift[...]
                parts.append(value / (1.0 + jnp.exp(-value)))
            value = jnp.where(inside, jnp.concatenate(parts, axis=0), 0.0)
            m.cells[phase * 96 : phase * 96 + 96, :] = value.astype(jnp.bfloat16)

    load_decode.wait()
    for tap in range(9):
        value = jnp.dot(m.cells[...], m.decode_in[tap], preferred_element_type=jnp.float32)
        m.products[tap] = value.reshape(4, 4, 3, 8, 256)

    for a in range(2):
        for b in range(2):
            for up in range(2):
                for left in range(2):
                    total = jnp.zeros((4, 2, 4, 256), jnp.float32) + m.decode_bias[...]
                    for di in range(3):
                        row_phase, row_at = phase_of(a, (up + di - 1) // 2)
                        for dj in range(3):
                            col_phase, col_at = phase_of(b, (left + dj - 1) // 2)
                            total += m.products[
                                di * 3 + dj,
                                row_phase * 2 + col_phase,
                                :,
                                row_at : row_at + 2,
                                col_at : col_at + 4,
                                :,
                            ]
                    for mb in range(4):
                        for i in range(2):
                            for half in range(2):
                                m.staged[
                                    half,
                                    mb,
                                    4 * i + 2 * a + up,
                                    pl.ds(2 * b + left, 4, stride=4),
                                    :,
                                ] = total[mb, i, :, half * 128 : half * 128 + 128]
    stores = [
        load(m.staged.at[half], m.out.at[:, :, :, pl.ds(half * 128, 128)], half)
        for half in range(2)
    ]
    for copy in stores:
        copy.wait()

    for copy in from_partner:
        copy.wait_send()
    for copy in ring.values():
        copy.wait_send()
    for copy in sent:
        copy.wait_send()
    for copy in sib_copies.values():
        copy.wait_send()
    for copy in sum_copies.values():
        copy.wait_send()


def shards(*args):
    shapes = {
        "latent_bias": (1, 512),
        "gain": (1, 512),
        "shift": (1, 512),
        "decode_kernel": (9, 512, 256),
        "decode_bias": (1, 256),
    }
    turned = {"modulation": (1, 0, 2), "reduce": (1, 0), "patch": (1, 0)}
    args = [
        a.transpose(turned[name]) if name in turned else a.reshape(shapes.get(name, a.shape))
        for name, a in zip(INPUTS, args, strict=True)
    ]
    return pl.pallas_call(
        program_kernel,
        out_shape=jax.ShapeDtypeStruct((4, 8, 16, 256), F32),
        in_specs=[pl.BlockSpec(memory_space=space) for space in INPUTS.values()],
        out_specs=pl.BlockSpec(memory_space=pl.ANY),
        scratch_shapes=list(SCRATCH.values()),
        compiler_params=pltpu.CompilerParams(
            collective_id=0, has_side_effects=True, vmem_limit_bytes=56 * 2**20
        ),
    )(*args)


def solution(mesh):
    return jax.shard_map(
        shards,
        mesh=mesh,
        in_specs=(
            P(None, "row", "col"),
            P(),
            P(),
            P("row", "col"),
            P("col"),
            P("col", "row"),
            P("col"),
            P("col", None),
            P(),
            P(),
            P(),
            P(),
            P(),
            P(None, None, None, "section"),
            P("section"),
        ),
        out_specs=P(None, "row", "col", "section"),
        check_vma=False,
    )
```

```python
from types import SimpleNamespace

import jax
import jax.numpy as jnp
from jax import lax
from jax.experimental import pallas as pl
from jax.experimental.pallas import tpu as pltpu
from jax.sharding import PartitionSpec as P

MESH = pl.DeviceIdType.MESH
EPSILON = 1e-06
N_ROW = 16
N_COL = 8
CELLS = 64 * 64 * 16
WIDTH = 3072
BLOCK = 384
PIECE = 192
GROUPS = ((0, -1, 1), (-2, 2), (-3, 3), (4,))
OFFSETS = (0, -1, 1, -2, 2, -3, 3, 4)
BF16, F32 = jnp.bfloat16, jnp.float32
DMA = pltpu.SemaphoreType.DMA
INPUTS = {
    "tokens": pl.ANY,
    "order": pltpu.SMEM,
    "modulation": pl.ANY,
    "expand": pl.ANY,
    "expand_bias": pltpu.VMEM,
    "reduce": pl.ANY,
    "reduce_bias": pltpu.VMEM,
    "patch": pltpu.VMEM,
    "patch_bias": pltpu.VMEM,
    "latent_kernel": pl.ANY,
    "latent_bias": pltpu.VMEM,
    "gain": pltpu.VMEM,
    "shift": pltpu.VMEM,
    "decode_kernel": pl.ANY,
    "decode_bias": pltpu.VMEM,
}
SCRATCH = {
    "tokens_in": pltpu.VMEM((4, 64, BLOCK), F32),
    "factors": pltpu.VMEM((5, 4, WIDTH), F32),
    "latent_in": pltpu.VMEM((3, 3, 16, 512), F32),
    "decode_in": pltpu.VMEM((9, 512, 256), BF16),
    "tok": pltpu.VMEM((2, 128, BLOCK), F32),
    "first": pltpu.VMEM((3, 2, 2, 1, BLOCK), F32),
    "final": pltpu.VMEM((3, 8, 2, 1, BLOCK), F32),
    "normed": pltpu.VMEM((8, 2, 2, 128, BLOCK), BF16),
    "weights": pltpu.VMEM((8, 2, 2, PIECE, BLOCK), BF16),
    "total": pltpu.VMEM((512, BLOCK), F32),
    "hidden": pltpu.VMEM((2, 256, BLOCK), BF16),
    "based": pltpu.VMEM((2, 128, BLOCK), F32),
    "rows_in": pltpu.VMEM((8, 16, BLOCK), F32),
    "patch_all": pltpu.VMEM((8, BLOCK, 128), BF16),
    "stats": pltpu.VMEM((8, 8, 256), F32),
    "sib_out": pltpu.VMEM((8, 256, BLOCK), BF16),
    "sib_in": pltpu.VMEM((8, 256, BLOCK), BF16),
    "kept": pltpu.VMEM((8, 256, BLOCK), F32),
    "outgoing": pltpu.VMEM((8, 16, 16, BLOCK), BF16),
    "middle": pltpu.VMEM((7, 4, 4, 16, BLOCK), BF16),
    "second": pltpu.VMEM((7, 4, 16, BLOCK), BF16),
    "incoming": pltpu.VMEM((8, 16, 16, BLOCK), BF16),
    "residual": pltpu.VMEM((8, 2, 8, BLOCK), F32),
    "latents": pltpu.VMEM((16, 128), F32),
    "blocks": pltpu.VMEM((3, 3, 2, 16, 128), F32),
    "patches": pltpu.VMEM((4, 4, 16, 64), F32),
    "taps": pltpu.VMEM((2, 256, 2048), BF16),
    "act": pltpu.VMEM((4, 96, 512), F32),
    "cells": pltpu.VMEM((384, 512), BF16),
    "products": pltpu.VMEM((9, 4, 4, 3, 8, 256), F32),
    "col_stats": pltpu.VMEM((8, 8, 128), F32),
    "row_stats": pltpu.VMEM((16, 8, 128), F32),
    "staged": pltpu.VMEM((2, 4, 8, 16, 128), F32),
    "member": pltpu.VMEM((512, 128), BF16),
    "member_t": pltpu.VMEM((128, 512), BF16),
    "load_sem": DMA((8,)),
    "partner_send": DMA((2,)),
    "partner_recv": DMA((2,)),
    "ring_send": DMA((2, 2, 2, 4)),
    "ring_recv": DMA((2, 2, 2, 4)),
    "stat_send": DMA((8,)),
    "stat_recv": DMA((8,)),
    "base_send": DMA((8,)),
    "base_recv": DMA((8,)),
    "patch_send": DMA((2, 4)),
    "patch_recv": DMA((2, 4)),
    "tok_send": DMA((2, 4)),
    "tok_recv": DMA((2, 4)),
    "fwd_send": DMA((2, 4)),
    "fwd_recv": DMA((2, 4)),
    "sib_send": DMA((8,)),
    "sib_recv": DMA((8,)),
    "sum_send": DMA((4, 16)),
    "sum_recv": DMA((4, 16)),
    "halo_send": DMA((2, 3, 3)),
    "halo_recv": DMA((2, 3, 3)),
    "col_send": DMA((8,)),
    "col_recv": DMA((8,)),
    "row_send": DMA((16,)),
    "row_recv": DMA((16,)),
}


def phase_of(base, step):
    if base == 0:
        return [(1, 0), (0, 0), (1, 1)][step + 1]
    return [(0, 0), (1, 1), (0, 1)][step + 1]


def thirds(value):
    parts = []
    for _ in range(3):
        parts.append(value.astype(BF16))
        value = value - parts[-1].astype(F32)
    return jnp.concatenate(parts, axis=0)


def gathered(value, member):
    product = jnp.dot(thirds(value), member, preferred_element_type=F32)
    return product[:8] + (product[8:16] + product[16:])


def program_kernel(*refs):
    names = [*INPUTS, "out", *SCRATCH]
    m = SimpleNamespace(**dict(zip(names, refs, strict=True)))
    s = lax.axis_index("section")
    r = lax.axis_index("row")
    c = lax.axis_index("col")
    z, yh = r // 2, r % 2
    x, k = c // 2, c % 2
    quarter = 2 * yh + s
    sibling = (s, r, 2 * x + 1 - k)
    partner = (1 - s, 2 * z + 1 - yh, c)

    def ring_place(step):
        return (s, 2 * lax.rem(z + step + 8, 8) + yh, c)

    def col_place(step):
        return (s, r, lax.rem(c + step, 8))

    def plane_place(dy, ds, dx):
        return (lax.rem(s + ds, 2), 2 * z + lax.rem(yh + dy, 2), 2 * lax.rem(x + dx, 4) + k)

    def send(source, target, send_sem, recv_sem, place):
        copy = pltpu.make_async_remote_copy(
            src_ref=source,
            dst_ref=target,
            send_sem=send_sem,
            recv_sem=recv_sem,
            device_id=place,
            device_id_type=MESH,
        )
        copy.start()
        return copy

    sent = []

    def place(ds, dr, dc):
        return (
            lax.rem(s + ds, 2),
            lax.rem(r + dr + N_ROW, N_ROW),
            lax.rem(c + dc + N_COL, N_COL),
        )

    halo = []
    for ds in range(2):
        for dr in (-1, 0, 1):
            for dc in (-1, 0, 1):
                if (ds, dr, dc) != (0, 0, 0):
                    halo.append((ds, dr, dc))

    barrier = pltpu.get_barrier_semaphore()
    greet = [place(0, step, 0) for step in range(1, N_ROW)]
    greet += [col_place(step) for step in range(1, N_COL)]
    for dy, ds in ((0, 1), (1, 0), (1, 1)):
        greet += [plane_place(dy, ds, dx) for dx in range(4)]
    greet += [place(*h) for h in halo if h[0] * (h[1] or h[2]) or h[1] * h[2]]
    for target in greet:
        pl.semaphore_signal(barrier, inc=1, device_id=target, device_id_type=MESH)

    def load(source, target, index):
        copy = pltpu.make_async_copy(source, target, m.load_sem.at[index])
        copy.start()
        return copy

    own_cols = pl.ds(pl.multiple_of(quarter * BLOCK, BLOCK), BLOCK)
    other_cols = pl.ds(pl.multiple_of((3 - quarter) * BLOCK, BLOCK), BLOCK)
    load_expand = load(m.expand.at[:, own_cols], m.weights.at[z, 0, yh], 0)
    load_tokens = load(m.tokens, m.tokens_in, 1)
    load_factors = load(m.modulation, m.factors, 2)
    load_reduce = [
        load(m.reduce.at[:, own_cols], m.weights.at[z, 1, yh], 3),
    ]
    load_latent = load(m.latent_kernel, m.latent_in, 5)
    load_decode = load(m.decode_kernel, m.decode_in, 6)

    pl.semaphore_wait(barrier, len(greet))

    def to_partner(e, source):
        return send(
            source, m.weights.at[z, e, yh], m.partner_send.at[e], m.partner_recv.at[e], partner
        )

    ring = {}
    arrived = set()

    def ensure(e, o, way, d):
        if (e, o, way, d) not in arrived:
            ring[e, o, way, d].wait_recv()
            arrived.add((e, o, way, d))

    def reach(o, way):
        return 4 if (o == 0) == (way == 1) else 3

    def ring_step(e, d, units=(0, 1)):
        for o in units:
            half = lax.rem(yh + o, 2)
            for way in (1, -1):
                if d > reach(o, way):
                    continue
                if d > 1:
                    ensure(e, o, way, d - 1)
                held = m.weights.at[lax.rem(z - way * (d - 1) + 8, 8), e, half]
                index = (1 - way) // 2
                ring[e, o, way, d] = send(
                    held,
                    held,
                    m.ring_send.at[e, o, index, d - 1],
                    m.ring_recv.at[e, o, index, d - 1],
                    ring_place(way),
                )

    def arrive(e, d):
        for o in range(2):
            for way in (1, -1):
                if d <= reach(o, way):
                    ensure(e, o, way, d)

    load_expand.wait()
    ring_step(0, 1, (0,))
    from_partner = [to_partner(0, m.expand.at[:, other_cols])]

    load_tokens.wait()
    for slot in range(4):
        rows = m.tokens_in[m.order[slot]]
        for col in range(8):
            start = (slot // 2 * 4 + col // 2) * 16 + slot % 2 * 8
            m.tok[col % 2, start : start + 8, :] = jnp.concatenate(
                [rows[col * 4 : col * 4 + 4], rows[32 + col * 4 : 36 + col * 4]], axis=0
            )
    tok = m.tok[...].reshape(256, BLOCK)
    lane = lax.broadcasted_iota(jnp.int32, (256, 128), 1)
    token_sums = jnp.sum(tok, axis=1, keepdims=True)
    token_squares = jnp.sum(tok * tok, axis=1, keepdims=True)
    table = jnp.where(lane == 0, token_sums, jnp.where(lane == 1, token_squares, 0.0))
    m.stats[c] = table.T[:8]
    stat_copies = [
        send(m.stats.at[c], m.stats.at[c], m.stat_send.at[d], m.stat_recv.at[d], col_place(d))
        for d in range(1, 8)
    ]
    sent += stat_copies

    from_partner[0].wait_recv()
    ring_step(0, 1, (1,))

    load_factors.wait()
    lanes = pl.ds(pl.multiple_of(c * BLOCK, BLOCK), BLOCK)
    for slot in range(4):
        for j in range(3):
            m.first[j, slot // 2, slot % 2] = m.factors[j, pl.ds(m.order[slot], 1), lanes]

    source = lax.broadcasted_iota(jnp.int32, (64, 64), 0)
    target = lax.broadcasted_iota(jnp.int32, (64, 64), 1)
    swap = target == source % 4 * 16 + source // 4
    swap_bf16 = (source == target % 4 * 16 + target // 4).astype(F32).astype(BF16)
    patch_high = m.patch[...].astype(BF16)
    patch_low = (m.patch[...] - patch_high.astype(F32)).astype(BF16)
    m.patch_all[c] = jnp.concatenate(
        [jnp.dot(swap_bf16, part, preferred_element_type=F32) for part in (patch_high, patch_low)],
        axis=0,
    ).T.astype(BF16)
    patch_bias = jnp.dot(
        jnp.zeros((8, 64), F32) + m.patch_bias[...].reshape(1, 64),
        swap.astype(F32),
        preferred_element_type=F32,
        precision=lax.Precision.HIGHEST,
    )[:1]
    load_latent.wait()
    m.taps[...] = jnp.zeros_like(m.taps)
    for u in range(2):
        for v in range(2):
            for sa in range(2):
                for sb in range(2):
                    for a in range(2):
                        for b in range(2):
                            di = 2 * u + sa - 2 + a
                            dj = 2 * v + sb - 2 + b
                            if abs(di) <= 1 and abs(dj) <= 1:
                                row = ((u * 2 + v) * 2 + sa) * 2 + sb
                                tap = m.latent_in[di + 1, dj + 1]
                                high = tap.astype(jnp.bfloat16)
                                low = (tap - high.astype(jnp.float32)).astype(jnp.bfloat16)
                                phase = 2 * a + b
                                rows = pl.ds(row * 16, 16)
                                lanes = pl.ds(phase * 512, 512)
                                m.taps[0, rows, lanes] = high
                                m.taps[1, rows, lanes] = low
    m.patches[...] = jnp.zeros_like(m.patches)
    chan = lax.broadcasted_iota(jnp.int32, (512, 128), 0) // 16
    m.member[...] = (chan == lax.broadcasted_iota(jnp.int32, (512, 128), 1)).astype(F32).astype(BF16)
    chan_t = lax.broadcasted_iota(jnp.int32, (128, 512), 1) // 16
    m.member_t[...] = (chan_t == lax.broadcasted_iota(jnp.int32, (128, 512), 0)).astype(F32).astype(BF16)

    for slot in range(2):
        for j in range(3):
            for at in range(8):
                m.final[j, at, slot] = m.factors[
                    j + 2, pl.ds(m.order[2 * s + slot], 1), at * BLOCK : (at + 1) * BLOCK
                ]

    for copy in stat_copies:
        copy.wait_recv()
    ring_step(0, 2, (0,))
    table = jnp.concatenate([jnp.sum(m.stats[...], axis=0), jnp.zeros((120, 256), F32)], axis=0).T
    token_mean = table[:, 0:1] * (1.0 / WIDTH)
    token_scale = lax.rsqrt(table[:, 1:2] * (1.0 / WIDTH) - token_mean * token_mean + EPSILON)
    plain = (tok - token_mean) * token_scale
    for core in range(2):
        for group in range(8):
            start = core * 128 + group * 16
            part = plain[start : start + 16].reshape(2, 8, BLOCK)
            part = part * (1.0 + m.first[1, group // 4]) + m.first[0, group // 4]
            m.normed[c, core, yh, pl.ds(group * 16, 16), :] = part.reshape(16, BLOCK).astype(BF16)

    tok_copies = {}

    def share(dy, dx, col, half, target):
        piece = m.normed.at[col, :, half]
        tok_copies[dy, dx] = send(
            piece, piece, m.tok_send.at[dy, dx], m.tok_recv.at[dy, dx], target
        )

    share(1, 0, c, yh, partner)
    for dx in (3, 1, 2):
        share(0, dx, c, yh, plane_place(0, 0, dx))
    share(0, 0, c, yh, sibling)

    ring_step(0, 2, (1,))

    for copy in load_reduce:
        copy.wait()
    from_partner.append(to_partner(1, m.reduce.at[:, other_cols]))

    for core in range(2):
        for group in range(8):
            rows = pl.ds(group * 16, 16)
            part = m.tok[core, rows, :].reshape(2, 8, BLOCK)
            part = part + m.first[2, group // 4] * m.reduce_bias[...].reshape(1, BLOCK)
            m.based[core, rows, :] = part.reshape(16, BLOCK)
    base_copies = []
    for d in range(1, 8):
        target = lax.rem(c + d, 8)
        rows = pl.ds(pl.multiple_of((s * 4 + target // 2) * 16, 16), 16)
        base_copies.append(
            send(
                m.based.at[target % 2, rows, :],
                m.rows_in.at[c],
                m.base_send.at[d],
                m.base_recv.at[d],
                col_place(d),
            )
        )
    sent += base_copies
    own_rows = pl.ds(pl.multiple_of((s * 4 + x) * 16, 16), 16)
    m.rows_in[c] = m.based[k, own_rows, :]

    forwards = []

    def forward(dy, dx):
        tok_copies[dy, dx].wait_recv()
        col, half = 2 * lax.rem(x - dx + 4, 4) + k, lax.rem(yh + dy, 2)
        if (dy, dx) == (1, 0):
            share(1, 1, col, half, plane_place(0, 0, 1))
        if dy == 0 and dx > 1:
            share(1, dx, col, half, partner)
        piece = m.normed.at[col, :, half]
        forwards.append(send(piece, piece, m.fwd_send.at[dy, dx], m.fwd_recv.at[dy, dx], sibling))

    for dy, dx in ((1, 0), (0, 3), (0, 1)):
        forward(dy, dx)
    ring_step(0, 3)
    for dy, dx in ((0, 2), (1, 1), (1, 3)):
        forward(dy, dx)
    ring_step(0, 4)
    from_partner[1].wait_recv()
    ring_step(1, 1)
    forward(1, 2)
    sent += forwards
    sent += tok_copies.values()

    patch_copies = [
        send(
            m.patch_all.at[c],
            m.patch_all.at[c],
            m.patch_send.at[0, d],
            m.patch_recv.at[0, d],
            plane_place(0, 0, d) if d else sibling,
        )
        for d in (1, 3, 2, 0)
    ]
    sent += patch_copies

    tok_copies[0, 0].wait_recv()
    for copy in forwards:
        copy.wait_recv()

    def expand(offset):
        at = lax.rem(z + offset + 8, 8)
        value = jnp.dot(
            m.normed[at].reshape(512, BLOCK),
            m.weights[at, 0].reshape(BLOCK, BLOCK),
            preferred_element_type=F32,
        )
        if offset == 0:
            m.total[...] = value
        else:
            m.total[...] += value

    arrive(0, 2)
    for offset in OFFSETS[:5]:
        expand(offset)
    arrive(0, 3)
    expand(-3)
    expand(3)
    arrive(0, 4)
    expand(4)
    value = m.total[...] + m.expand_bias[own_cols].reshape(1, BLOCK)
    inner = 0.7978845608028654 * (value + 0.044715 * (value * value * value))
    value = 0.5 * value * (1.0 + jnp.tanh(inner))
    m.hidden[...] = value.astype(BF16).reshape(2, 256, BLOCK)

    sib_copies = {}

    def contract(offset):
        slot = OFFSETS.index(offset)
        at = lax.rem(z + offset + 8, 8)
        right = m.weights[at, 1].reshape(BLOCK, BLOCK)
        away = lax.dot_general(
            m.hidden[1 - k], right, (((1,), (1,)), ((), ())), preferred_element_type=F32
        )
        m.sib_out[slot] = away.astype(BF16)
        sib_copies[slot] = send(
            m.sib_out.at[slot],
            m.sib_in.at[slot],
            m.sib_send.at[slot],
            m.sib_recv.at[slot],
            sibling,
        )
        m.kept[slot] = lax.dot_general(
            m.hidden[k], right, (((1,), (1,)), ((), ())), preferred_element_type=F32
        )

    m_own = yh * 8 + s * 4 + x
    sum_copies = {}

    def scatter(g):
        first_slot = OFFSETS.index(GROUPS[g][0])
        count = len(GROUPS[g])
        for slot in range(first_slot, first_slot + count):
            sib_copies[slot].wait_recv()
            value = m.kept[slot] + m.sib_in[slot].astype(F32)
            m.outgoing[slot] = value.astype(BF16).reshape(16, 16, BLOCK)
        slots = pl.ds(first_slot, count)
        for dx in (2, 1, 3, 0):
            for dy in range(2):
                for ds in range(2):
                    if (dy, ds, dx) == (0, 0, 0):
                        continue
                    there = plane_place(dy, ds, dx)
                    m_there = lax.rem(yh + dy, 2) * 8 + there[0] * 4 + lax.rem(x + dx, 4)
                    index = dy * 8 + ds * 4 + dx
                    sum_copies[g, index] = send(
                        m.outgoing.at[slots, m_there],
                        m.incoming.at[slots, m_own],
                        m.sum_send.at[g, index],
                        m.sum_recv.at[g, index],
                        there,
                    )
        m.incoming[slots, m_own] = m.outgoing[slots, m_own]

    row_parts = []

    def collect(g):
        for index in range(1, 16):
            sum_copies[g, index].wait_recv()
        for offset in GROUPS[g]:
            slot = OFFSETS.index(offset)
            at = lax.rem(z + offset + 8, 8)
            branch = jnp.sum(m.incoming[slot].astype(F32), axis=0).reshape(2, 8, BLOCK)
            value = m.rows_in[at].reshape(2, 8, BLOCK) + m.final[0, at] * branch
            m.residual[slot] = value
            row_parts.append(
                (
                    jnp.sum(value, axis=2, keepdims=True),
                    jnp.sum(value * value, axis=2, keepdims=True),
                )
            )

    contract(0)
    ring_step(1, 2)
    arrive(1, 1)
    contract(-1)
    contract(1)
    scatter(0)
    patch_forwards = []
    for d, copy in zip((1, 3, 2), patch_copies):
        copy.wait_recv()
        piece = m.patch_all.at[2 * lax.rem(x - d + 4, 4) + k]
        patch_forwards.append(
            send(piece, piece, m.patch_send.at[1, d], m.patch_recv.at[1, d], sibling)
        )
    sent += patch_forwards
    ring_step(1, 3)
    arrive(1, 2)
    contract(-2)
    contract(2)
    scatter(1)
    ring_step(1, 4)
    for copy in base_copies:
        copy.wait_recv()
    arrive(1, 3)
    contract(-3)
    contract(3)
    scatter(2)
    collect(0)
    arrive(1, 4)
    contract(4)
    scatter(3)
    for g in range(1, 4):
        collect(g)
    row_sums = sum(part[0] for part in row_parts)
    row_squares = sum(part[1] for part in row_parts)
    row_mean = row_sums * (1.0 / WIDTH)
    row_scale = lax.rsqrt(row_squares * (1.0 / WIDTH) - row_mean * row_mean + EPSILON)
    for copy in (patch_copies[3], *patch_forwards):
        copy.wait_recv()
    projected = jnp.zeros((32, 128), F32)
    for slot in range(8):
        at = lax.rem(z + OFFSETS[slot] + 8, 8)
        value = (m.residual[slot] - row_mean) * row_scale * (1.0 + m.final[2, at]) + m.final[1, at]
        value = value.reshape(16, BLOCK)
        high = value.astype(BF16)
        low = (value - high.astype(F32)).astype(BF16)
        projected += jnp.dot(
            jnp.concatenate([high, low], axis=0), m.patch_all[at], preferred_element_type=F32
        )
    patch = projected[:16, :64] + (projected[16:, :64] + projected[:16, 64:])
    latent = (patch + patch_bias) / 0.3611 + 0.1159
    latent = jnp.concatenate([latent, jnp.zeros((16, 64), F32)], axis=1)
    m.latents[...] = latent
    m.blocks[1, 1, s] = latent

    copies = []
    for ds, dr, dc in halo:
        copy = pltpu.make_async_remote_copy(
            src_ref=m.latents,
            dst_ref=m.blocks.at[1 - dr, 1 - dc, s],
            send_sem=m.halo_send.at[ds, 1 - dr, 1 - dc],
            recv_sem=m.halo_recv.at[ds, 1 - dr, 1 - dc],
            device_id=place(ds, dr, dc),
            device_id_type=MESH,
        )
        copy.start()
        copies.append(copy)

    for copy in copies:
        copy.wait_recv()
    sent += copies

    for ds in range(2):
        for dr in (-1, 0, 1):
            for dc in (-1, 0, 1):
                inside = (r + dr >= 0) & (r + dr < N_ROW) & (c + dc >= 0) & (c + dc < N_COL)
                keep = jnp.where(inside, 1.0, 0.0).astype(jnp.float32)
                block = m.blocks[dr + 1, dc + 1, ds][:, :64] * keep
                rows = {-1: ((1, 0),), 0: ((0, 1), (1, 2)), 1: ((0, 3),)}[dr]
                first, count, at = {-1: (3, 1, 0), 0: (0, 4, 1), 1: (0, 1, 5)}[dc]
                for mb in range(2):
                    for source, target in rows:
                        start = mb * 8 + source * 4 + first
                        m.patches[2 * ds + mb, target, at : at + count, :] = block[
                            start : start + count
                        ]

    slabs = [
        m.patches[:, u : u + 3, v : v + 8, :].reshape(96, 64) for u in range(2) for v in range(2)
    ]
    window = jnp.concatenate(slabs, axis=-1)
    high = window.astype(jnp.bfloat16)
    low = (window - high.astype(jnp.float32)).astype(jnp.bfloat16)
    both = jnp.concatenate([high, low], axis=0)

    jj = lax.broadcasted_iota(jnp.int32, (96, 1), 0) % 8
    ii = (lax.broadcasted_iota(jnp.int32, (96, 1), 0) // 8) % 3
    sums = jnp.zeros((4, 512), jnp.float32)
    squares = jnp.zeros((4, 512), jnp.float32)
    for a in range(2):
        for b in range(2):
            phase = 2 * a + b
            lanes = pl.ds(phase * 512, 512)
            first = jnp.dot(both, m.taps[0, :, lanes], preferred_element_type=jnp.float32)
            second = jnp.dot(high, m.taps[1, :, lanes], preferred_element_type=jnp.float32)
            value = first[:96] + (first[96:] + second) + m.latent_bias[...]
            m.act[phase] = value
            own = (ii >= a) & (ii < a + 2) & (jj >= b) & (jj < b + 4)
            masked = jnp.where(own, value, 0.0).reshape(4, 24, 512)
            sums += jnp.sum(masked, axis=1)
            squares += jnp.sum(masked * masked, axis=1)

    stats = gathered(jnp.concatenate([sums, squares], axis=0), m.member[...])

    m.col_stats[c] = stats
    copies = []
    for dc in range(1, N_COL):
        copy = pltpu.make_async_remote_copy(
            src_ref=m.col_stats.at[c],
            dst_ref=m.col_stats.at[c],
            send_sem=m.col_send.at[dc],
            recv_sem=m.col_recv.at[dc],
            device_id=place(0, 0, dc),
            device_id_type=MESH,
        )
        copy.start()
        copies.append(copy)
    for copy in copies:
        copy.wait_recv()
    sent += copies
    m.row_stats[r] = jnp.sum(m.col_stats[...], axis=0)
    copies = []
    for dr in range(1, N_ROW):
        copy = pltpu.make_async_remote_copy(
            src_ref=m.row_stats.at[r],
            dst_ref=m.row_stats.at[r],
            send_sem=m.row_send.at[dr],
            recv_sem=m.row_recv.at[dr],
            device_id=place(0, dr, 0),
            device_id_type=MESH,
        )
        copy.start()
        copies.append(copy)
    for copy in copies:
        copy.wait_recv()
    sent += copies
    total = jnp.sum(m.row_stats[...], axis=0) * (1.0 / CELLS)
    mean = total[:4]
    scale = lax.rsqrt(total[4:] - mean * mean + EPSILON)
    spread = gathered(jnp.concatenate([mean, scale], axis=0), m.member_t[...])

    for a in range(2):
        for b in range(2):
            phase = 2 * a + b
            line = 4 * r + 2 * ii - a
            across = 8 * c + 2 * jj - b
            inside = (line >= 0) & (line < 64) & (across >= 0) & (across < 64)
            parts = []
            for mb in range(4):
                value = m.act[phase, mb * 24 : mb * 24 + 24]
                value = (value - spread[mb : mb + 1]) * (
                    spread[4 + mb : 5 + mb] * m.gain[...]
                ) + m.shift[...]
                parts.append(value / (1.0 + jnp.exp(-value)))
            value = jnp.where(inside, jnp.concatenate(parts, axis=0), 0.0)
            m.cells[phase * 96 : phase * 96 + 96, :] = value.astype(jnp.bfloat16)

    load_decode.wait()
    for tap in range(9):
        value = jnp.dot(m.cells[...], m.decode_in[tap], preferred_element_type=jnp.float32)
        m.products[tap] = value.reshape(4, 4, 3, 8, 256)

    for a in range(2):
        for b in range(2):
            for up in range(2):
                for left in range(2):
                    total = jnp.zeros((4, 2, 4, 256), jnp.float32) + m.decode_bias[...]
                    for di in range(3):
                        row_phase, row_at = phase_of(a, (up + di - 1) // 2)
                        for dj in range(3):
                            col_phase, col_at = phase_of(b, (left + dj - 1) // 2)
                            total += m.products[
                                di * 3 + dj,
                                row_phase * 2 + col_phase,
                                :,
                                row_at : row_at + 2,
                                col_at : col_at + 4,
                                :,
                            ]
                    for mb in range(4):
                        for i in range(2):
                            for half in range(2):
                                m.staged[
                                    half,
                                    mb,
                                    4 * i + 2 * a + up,
                                    pl.ds(2 * b + left, 4, stride=4),
                                    :,
                                ] = total[mb, i, :, half * 128 : half * 128 + 128]
    stores = [
        load(m.staged.at[half], m.out.at[:, :, :, pl.ds(half * 128, 128)], half)
        for half in range(2)
    ]
    for copy in stores:
        copy.wait()

    for copy in from_partner:
        copy.wait_send()
    for copy in ring.values():
        copy.wait_send()
    for copy in sent:
        copy.wait_send()
    for copy in sib_copies.values():
        copy.wait_send()
    for copy in sum_copies.values():
        copy.wait_send()


def shards(*args):
    shapes = {
        "latent_bias": (1, 512),
        "gain": (1, 512),
        "shift": (1, 512),
        "decode_kernel": (9, 512, 256),
        "decode_bias": (1, 256),
    }
    turned = {"modulation": (1, 0, 2), "reduce": (1, 0), "patch": (1, 0)}
    args = [
        a.transpose(turned[name]) if name in turned else a.reshape(shapes.get(name, a.shape))
        for name, a in zip(INPUTS, args, strict=True)
    ]
    return pl.pallas_call(
        program_kernel,
        out_shape=jax.ShapeDtypeStruct((4, 8, 16, 256), F32),
        in_specs=[pl.BlockSpec(memory_space=space) for space in INPUTS.values()],
        out_specs=pl.BlockSpec(memory_space=pl.ANY),
        scratch_shapes=list(SCRATCH.values()),
        compiler_params=pltpu.CompilerParams(
            collective_id=0, has_side_effects=True, vmem_limit_bytes=56 * 2**20
        ),
    )(*args)


def solution(mesh):
    return jax.shard_map(
        shards,
        mesh=mesh,
        in_specs=(
            P(None, "row", "col"),
            P(),
            P(),
            P("row", "col"),
            P("col"),
            P("col", "row"),
            P("col"),
            P("col", None),
            P(),
            P(),
            P(),
            P(),
            P(),
            P(None, None, None, "section"),
            P("section"),
        ),
        out_specs=P(None, "row", "col", "section"),
        check_vma=False,
    )
```

```python
from types import SimpleNamespace

import jax
import jax.numpy as jnp
from jax import lax
from jax.experimental import pallas as pl
from jax.experimental.pallas import tpu as pltpu
from jax.sharding import PartitionSpec as P

MESH = pl.DeviceIdType.MESH
EPSILON = 1e-06
N_ROW = 16
N_COL = 8
CELLS = 64 * 64 * 16
WIDTH = 3072
BLOCK = 384
PIECE = 192
GROUPS = ((0, -1, 1), (-2, 2), (-3, 3), (4,))
OFFSETS = (0, -1, 1, -2, 2, -3, 3, 4)
BF16, F32 = jnp.bfloat16, jnp.float32
DMA = pltpu.SemaphoreType.DMA
INPUTS = {
    "tokens": pltpu.HBM,
    "order": pltpu.SMEM,
    "modulation": pltpu.HBM,
    "expand": pltpu.HBM,
    "expand_bias": pltpu.HBM,
    "reduce": pltpu.HBM,
    "reduce_bias": pltpu.HBM,
    "patch": pltpu.HBM,
    "patch_bias": pltpu.HBM,
    "latent_kernel": pltpu.HBM,
    "latent_bias": pltpu.HBM,
    "gain": pltpu.HBM,
    "shift": pltpu.HBM,
    "decode_kernel": pltpu.HBM,
    "decode_bias": pltpu.HBM,
}
SMALL = {
    "expand_bias": (1536,),
    "reduce_bias": (BLOCK,),
    "patch": (64, BLOCK),
    "patch_bias": (64,),
    "latent_bias": (1, 512),
    "gain": (1, 512),
    "shift": (1, 512),
    "decode_bias": (1, 256),
}
SCRATCH = {
    "tokens_in": pltpu.VMEM((4, 64, BLOCK), F32),
    "factors": pltpu.VMEM((5, 4, WIDTH), F32),
    "latent_in": pltpu.VMEM((3, 3, 16, 512), F32),
    "decode_in": pltpu.VMEM((9, 512, 256), BF16),
    "tok": pltpu.VMEM((2, 128, BLOCK), F32),
    "first": pltpu.VMEM((3, 2, 2, 1, BLOCK), F32),
    "final": pltpu.VMEM((3, 8, 2, 1, BLOCK), F32),
    "normed": pltpu.VMEM((8, 2, 2, 128, BLOCK), BF16),
    "weights": pltpu.VMEM((8, 2, 2, PIECE, BLOCK), BF16),
    "total": pltpu.VMEM((512, BLOCK), F32),
    "hidden": pltpu.VMEM((2, 256, BLOCK), BF16),
    "based": pltpu.VMEM((2, 128, BLOCK), F32),
    "rows_in": pltpu.VMEM((8, 16, BLOCK), F32),
    "patch_all": pltpu.VMEM((8, BLOCK, 128), BF16),
    "stats": pltpu.VMEM((8, 8, 256), F32),
    "sib_out": pltpu.VMEM((8, 256, BLOCK), BF16),
    "sib_in": pltpu.VMEM((8, 256, BLOCK), BF16),
    "kept": pltpu.VMEM((8, 256, BLOCK), F32),
    "outgoing": pltpu.VMEM((8, 16, 16, BLOCK), BF16),
    "middle": pltpu.VMEM((7, 4, 4, 16, BLOCK), BF16),
    "second": pltpu.VMEM((7, 4, 16, BLOCK), BF16),
    "incoming": pltpu.VMEM((8, 16, 16, BLOCK), BF16),
    "residual": pltpu.VMEM((8, 2, 8, BLOCK), F32),
    "latents": pltpu.VMEM((16, 128), F32),
    "blocks": pltpu.VMEM((3, 3, 2, 16, 128), F32),
    "patches": pltpu.VMEM((4, 4, 16, 64), F32),
    "taps": pltpu.VMEM((2, 256, 2048), BF16),
    "act": pltpu.VMEM((4, 96, 512), F32),
    "cells": pltpu.VMEM((384, 512), BF16),
    "products": pltpu.VMEM((9, 4, 4, 3, 8, 256), F32),
    "col_stats": pltpu.VMEM((8, 8, 128), F32),
    "row_stats": pltpu.VMEM((16, 8, 128), F32),
    "staged": pltpu.VMEM((2, 4, 8, 16, 128), F32),
    "member": pltpu.VMEM((512, 128), BF16),
    "member_t": pltpu.VMEM((128, 512), BF16),
    **{name + "_in": pltpu.VMEM(shape, F32) for name, shape in SMALL.items()},
    "load_sem": DMA((16,)),
    "partner_send": DMA((2,)),
    "partner_recv": DMA((2,)),
    "ring_send": DMA((2, 2, 2, 4)),
    "ring_recv": DMA((2, 2, 2, 4)),
    "stat_send": DMA((8,)),
    "stat_recv": DMA((8,)),
    "base_send": DMA((8,)),
    "base_recv": DMA((8,)),
    "patch_send": DMA((2, 4)),
    "patch_recv": DMA((2, 4)),
    "tok_send": DMA((2, 4)),
    "tok_recv": DMA((2, 4)),
    "fwd_send": DMA((2, 4)),
    "fwd_recv": DMA((2, 4)),
    "sib_send": DMA((8,)),
    "sib_recv": DMA((8,)),
    "sum_send": DMA((4, 16)),
    "sum_recv": DMA((4, 16)),
    "halo_send": DMA((2, 3, 3)),
    "halo_recv": DMA((2, 3, 3)),
    "col_send": DMA((8,)),
    "col_recv": DMA((8,)),
    "row_send": DMA((16,)),
    "row_recv": DMA((16,)),
}


def phase_of(base, step):
    if base == 0:
        return [(1, 0), (0, 0), (1, 1)][step + 1]
    return [(0, 0), (1, 1), (0, 1)][step + 1]


def thirds(value):
    parts = []
    for _ in range(3):
        parts.append(value.astype(BF16))
        value = value - parts[-1].astype(F32)
    return jnp.concatenate(parts, axis=0)


def gathered(value, member):
    product = jnp.dot(thirds(value), member, preferred_element_type=F32)
    return product[:8] + (product[8:16] + product[16:])


def program_kernel(*refs):
    names = [*INPUTS, "out", *SCRATCH]
    m = SimpleNamespace(**dict(zip(names, refs, strict=True)))
    s = lax.axis_index("section")
    r = lax.axis_index("row")
    c = lax.axis_index("col")
    z, yh = r // 2, r % 2
    x, k = c // 2, c % 2
    quarter = 2 * yh + s
    sibling = (s, r, 2 * x + 1 - k)
    partner = (1 - s, 2 * z + 1 - yh, c)

    def ring_place(step):
        return (s, 2 * lax.rem(z + step + 8, 8) + yh, c)

    def col_place(step):
        return (s, r, lax.rem(c + step, 8))

    def plane_place(dy, ds, dx):
        return (lax.rem(s + ds, 2), 2 * z + lax.rem(yh + dy, 2), 2 * lax.rem(x + dx, 4) + k)

    def send(source, target, send_sem, recv_sem, place):
        copy = pltpu.make_async_remote_copy(
            src_ref=source,
            dst_ref=target,
            send_sem=send_sem,
            recv_sem=recv_sem,
            device_id=place,
            device_id_type=MESH,
        )
        copy.start()
        return copy

    sent = []

    def place(ds, dr, dc):
        return (
            lax.rem(s + ds, 2),
            lax.rem(r + dr + N_ROW, N_ROW),
            lax.rem(c + dc + N_COL, N_COL),
        )

    halo = []
    for ds in range(2):
        for dr in (-1, 0, 1):
            for dc in (-1, 0, 1):
                if (ds, dr, dc) != (0, 0, 0):
                    halo.append((ds, dr, dc))

    barrier = pltpu.get_barrier_semaphore()
    greet = [place(0, step, 0) for step in range(1, N_ROW)]
    greet += [col_place(step) for step in range(1, N_COL)]
    for dy, ds in ((0, 1), (1, 0), (1, 1)):
        greet += [plane_place(dy, ds, dx) for dx in range(4)]
    greet += [place(*h) for h in halo if h[0] * (h[1] or h[2]) or h[1] * h[2]]
    for target in greet:
        pl.semaphore_signal(barrier, inc=1, device_id=target, device_id_type=MESH)

    def load(source, target, index):
        copy = pltpu.make_async_copy(source, target, m.load_sem.at[index])
        copy.start()
        return copy

    own_cols = pl.ds(pl.multiple_of(quarter * BLOCK, BLOCK), BLOCK)
    other_cols = pl.ds(pl.multiple_of((3 - quarter) * BLOCK, BLOCK), BLOCK)
    load_expand = load(m.expand.at[:, own_cols], m.weights.at[z, 0, yh], 0)
    load_tokens = load(m.tokens, m.tokens_in, 1)
    load_factors = load(m.modulation, m.factors, 2)
    load_reduce = [
        load(m.reduce.at[:, own_cols], m.weights.at[z, 1, yh], 3),
    ]
    load_latent = load(m.latent_kernel, m.latent_in, 5)
    small = []
    for index, name in enumerate(SMALL):
        held = getattr(m, name + "_in")
        small.append(load(getattr(m, name), held, 8 + index))
        setattr(m, name, held)
    load_decode = load(m.decode_kernel, m.decode_in, 6)

    pl.semaphore_wait(barrier, len(greet))

    def to_partner(e, source):
        return send(
            source, m.weights.at[z, e, yh], m.partner_send.at[e], m.partner_recv.at[e], partner
        )

    ring = {}
    arrived = set()

    def ensure(e, o, way, d):
        if (e, o, way, d) not in arrived:
            ring[e, o, way, d].wait_recv()
            arrived.add((e, o, way, d))

    def reach(o, way):
        return 4 if (o == 0) == (way == 1) else 3

    def ring_step(e, d, units=(0, 1)):
        for o in units:
            half = lax.rem(yh + o, 2)
            for way in (1, -1):
                if d > reach(o, way):
                    continue
                if d > 1:
                    ensure(e, o, way, d - 1)
                held = m.weights.at[lax.rem(z - way * (d - 1) + 8, 8), e, half]
                index = (1 - way) // 2
                ring[e, o, way, d] = send(
                    held,
                    held,
                    m.ring_send.at[e, o, index, d - 1],
                    m.ring_recv.at[e, o, index, d - 1],
                    ring_place(way),
                )

    def arrive(e, d):
        for o in range(2):
            for way in (1, -1):
                if d <= reach(o, way):
                    ensure(e, o, way, d)

    load_expand.wait()
    ring_step(0, 1, (0,))
    for copy in small:
        copy.wait()
    from_partner = [to_partner(0, m.expand.at[:, other_cols])]

    load_tokens.wait()
    for slot in range(4):
        rows = m.tokens_in[m.order[slot]]
        for col in range(8):
            start = (slot // 2 * 4 + col // 2) * 16 + slot % 2 * 8
            m.tok[col % 2, start : start + 8, :] = jnp.concatenate(
                [rows[col * 4 : col * 4 + 4], rows[32 + col * 4 : 36 + col * 4]], axis=0
            )
    tok = m.tok[...].reshape(256, BLOCK)
    lane = lax.broadcasted_iota(jnp.int32, (256, 128), 1)
    token_sums = jnp.sum(tok, axis=1, keepdims=True)
    token_squares = jnp.sum(tok * tok, axis=1, keepdims=True)
    table = jnp.where(lane == 0, token_sums, jnp.where(lane == 1, token_squares, 0.0))
    m.stats[c] = table.T[:8]
    stat_copies = [
        send(m.stats.at[c], m.stats.at[c], m.stat_send.at[d], m.stat_recv.at[d], col_place(d))
        for d in range(1, 8)
    ]
    sent += stat_copies

    from_partner[0].wait_recv()
    ring_step(0, 1, (1,))

    load_factors.wait()
    lanes = pl.ds(pl.multiple_of(c * BLOCK, BLOCK), BLOCK)
    for slot in range(4):
        for j in range(3):
            m.first[j, slot // 2, slot % 2] = m.factors[j, pl.ds(m.order[slot], 1), lanes]

    source = lax.broadcasted_iota(jnp.int32, (64, 64), 0)
    target = lax.broadcasted_iota(jnp.int32, (64, 64), 1)
    swap = target == source % 4 * 16 + source // 4
    swap_bf16 = (source == target % 4 * 16 + target // 4).astype(F32).astype(BF16)
    patch_high = m.patch[...].astype(BF16)
    patch_low = (m.patch[...] - patch_high.astype(F32)).astype(BF16)
    m.patch_all[c] = jnp.concatenate(
        [jnp.dot(swap_bf16, part, preferred_element_type=F32) for part in (patch_high, patch_low)],
        axis=0,
    ).T.astype(BF16)
    patch_bias = jnp.dot(
        jnp.zeros((8, 64), F32) + m.patch_bias[...].reshape(1, 64),
        swap.astype(F32),
        preferred_element_type=F32,
        precision=lax.Precision.HIGHEST,
    )[:1]
    load_latent.wait()
    m.taps[...] = jnp.zeros_like(m.taps)
    for u in range(2):
        for v in range(2):
            for sa in range(2):
                for sb in range(2):
                    for a in range(2):
                        for b in range(2):
                            di = 2 * u + sa - 2 + a
                            dj = 2 * v + sb - 2 + b
                            if abs(di) <= 1 and abs(dj) <= 1:
                                row = ((u * 2 + v) * 2 + sa) * 2 + sb
                                tap = m.latent_in[di + 1, dj + 1]
                                high = tap.astype(jnp.bfloat16)
                                low = (tap - high.astype(jnp.float32)).astype(jnp.bfloat16)
                                phase = 2 * a + b
                                rows = pl.ds(row * 16, 16)
                                lanes = pl.ds(phase * 512, 512)
                                m.taps[0, rows, lanes] = high
                                m.taps[1, rows, lanes] = low
    m.patches[...] = jnp.zeros_like(m.patches)
    chan = lax.broadcasted_iota(jnp.int32, (512, 128), 0) // 16
    m.member[...] = (chan == lax.broadcasted_iota(jnp.int32, (512, 128), 1)).astype(F32).astype(BF16)
    chan_t = lax.broadcasted_iota(jnp.int32, (128, 512), 1) // 16
    m.member_t[...] = (chan_t == lax.broadcasted_iota(jnp.int32, (128, 512), 0)).astype(F32).astype(BF16)

    for slot in range(2):
        for j in range(3):
            for at in range(8):
                m.final[j, at, slot] = m.factors[
                    j + 2, pl.ds(m.order[2 * s + slot], 1), at * BLOCK : (at + 1) * BLOCK
                ]

    for copy in stat_copies:
        copy.wait_recv()
    ring_step(0, 2, (0,))
    table = jnp.concatenate([jnp.sum(m.stats[...], axis=0), jnp.zeros((120, 256), F32)], axis=0).T
    token_mean = table[:, 0:1] * (1.0 / WIDTH)
    token_scale = lax.rsqrt(table[:, 1:2] * (1.0 / WIDTH) - token_mean * token_mean + EPSILON)
    plain = (tok - token_mean) * token_scale
    for core in range(2):
        for group in range(8):
            start = core * 128 + group * 16
            part = plain[start : start + 16].reshape(2, 8, BLOCK)
            part = part * (1.0 + m.first[1, group // 4]) + m.first[0, group // 4]
            m.normed[c, core, yh, pl.ds(group * 16, 16), :] = part.reshape(16, BLOCK).astype(BF16)

    tok_copies = {}

    def share(dy, dx, col, half, target):
        piece = m.normed.at[col, :, half]
        tok_copies[dy, dx] = send(
            piece, piece, m.tok_send.at[dy, dx], m.tok_recv.at[dy, dx], target
        )

    share(1, 0, c, yh, partner)
    for dx in (3, 1, 2):
        share(0, dx, c, yh, plane_place(0, 0, dx))
    share(0, 0, c, yh, sibling)

    ring_step(0, 2, (1,))

    for copy in load_reduce:
        copy.wait()
    from_partner.append(to_partner(1, m.reduce.at[:, other_cols]))

    for core in range(2):
        for group in range(8):
            rows = pl.ds(group * 16, 16)
            part = m.tok[core, rows, :].reshape(2, 8, BLOCK)
            part = part + m.first[2, group // 4] * m.reduce_bias[...].reshape(1, BLOCK)
            m.based[core, rows, :] = part.reshape(16, BLOCK)
    base_copies = []
    for d in range(1, 8):
        target = lax.rem(c + d, 8)
        rows = pl.ds(pl.multiple_of((s * 4 + target // 2) * 16, 16), 16)
        base_copies.append(
            send(
                m.based.at[target % 2, rows, :],
                m.rows_in.at[c],
                m.base_send.at[d],
                m.base_recv.at[d],
                col_place(d),
            )
        )
    sent += base_copies
    own_rows = pl.ds(pl.multiple_of((s * 4 + x) * 16, 16), 16)
    m.rows_in[c] = m.based[k, own_rows, :]

    forwards = []

    def forward(dy, dx):
        tok_copies[dy, dx].wait_recv()
        col, half = 2 * lax.rem(x - dx + 4, 4) + k, lax.rem(yh + dy, 2)
        if (dy, dx) == (1, 0):
            share(1, 1, col, half, plane_place(0, 0, 1))
        if dy == 0 and dx > 1:
            share(1, dx, col, half, partner)
        piece = m.normed.at[col, :, half]
        forwards.append(send(piece, piece, m.fwd_send.at[dy, dx], m.fwd_recv.at[dy, dx], sibling))

    for dy, dx in ((1, 0), (0, 3), (0, 1)):
        forward(dy, dx)
    ring_step(0, 3)
    for dy, dx in ((0, 2), (1, 1), (1, 3)):
        forward(dy, dx)
    ring_step(0, 4)
    from_partner[1].wait_recv()
    ring_step(1, 1)
    forward(1, 2)
    sent += forwards
    sent += tok_copies.values()

    patch_copies = [
        send(
            m.patch_all.at[c],
            m.patch_all.at[c],
            m.patch_send.at[0, d],
            m.patch_recv.at[0, d],
            plane_place(0, 0, d) if d else sibling,
        )
        for d in (1, 3, 2, 0)
    ]
    sent += patch_copies

    tok_copies[0, 0].wait_recv()
    for copy in forwards:
        copy.wait_recv()

    def expand(offset):
        at = lax.rem(z + offset + 8, 8)
        value = jnp.dot(
            m.normed[at].reshape(512, BLOCK),
            m.weights[at, 0].reshape(BLOCK, BLOCK),
            preferred_element_type=F32,
        )
        if offset == 0:
            m.total[...] = value
        else:
            m.total[...] += value

    arrive(0, 2)
    for offset in OFFSETS[:5]:
        expand(offset)
    arrive(0, 3)
    expand(-3)
    expand(3)
    arrive(0, 4)
    expand(4)
    value = m.total[...] + m.expand_bias[own_cols].reshape(1, BLOCK)
    inner = 0.7978845608028654 * (value + 0.044715 * (value * value * value))
    value = 0.5 * value * (1.0 + jnp.tanh(inner))
    m.hidden[...] = value.astype(BF16).reshape(2, 256, BLOCK)

    sib_copies = {}

    def contract(offset):
        slot = OFFSETS.index(offset)
        at = lax.rem(z + offset + 8, 8)
        right = m.weights[at, 1].reshape(BLOCK, BLOCK)
        away = lax.dot_general(
            m.hidden[1 - k], right, (((1,), (1,)), ((), ())), preferred_element_type=F32
        )
        m.sib_out[slot] = away.astype(BF16)
        sib_copies[slot] = send(
            m.sib_out.at[slot],
            m.sib_in.at[slot],
            m.sib_send.at[slot],
            m.sib_recv.at[slot],
            sibling,
        )
        m.kept[slot] = lax.dot_general(
            m.hidden[k], right, (((1,), (1,)), ((), ())), preferred_element_type=F32
        )

    m_own = yh * 8 + s * 4 + x
    sum_copies = {}

    def scatter(g):
        first_slot = OFFSETS.index(GROUPS[g][0])
        count = len(GROUPS[g])
        for slot in range(first_slot, first_slot + count):
            sib_copies[slot].wait_recv()
            value = m.kept[slot] + m.sib_in[slot].astype(F32)
            m.outgoing[slot] = value.astype(BF16).reshape(16, 16, BLOCK)
        slots = pl.ds(first_slot, count)
        for dx in (2, 1, 3, 0):
            for dy in range(2):
                for ds in range(2):
                    if (dy, ds, dx) == (0, 0, 0):
                        continue
                    there = plane_place(dy, ds, dx)
                    m_there = lax.rem(yh + dy, 2) * 8 + there[0] * 4 + lax.rem(x + dx, 4)
                    index = dy * 8 + ds * 4 + dx
                    sum_copies[g, index] = send(
                        m.outgoing.at[slots, m_there],
                        m.incoming.at[slots, m_own],
                        m.sum_send.at[g, index],
                        m.sum_recv.at[g, index],
                        there,
                    )
        m.incoming[slots, m_own] = m.outgoing[slots, m_own]

    row_parts = []

    def collect(g):
        for index in range(1, 16):
            sum_copies[g, index].wait_recv()
        for offset in GROUPS[g]:
            slot = OFFSETS.index(offset)
            at = lax.rem(z + offset + 8, 8)
            branch = jnp.sum(m.incoming[slot].astype(F32), axis=0).reshape(2, 8, BLOCK)
            value = m.rows_in[at].reshape(2, 8, BLOCK) + m.final[0, at] * branch
            m.residual[slot] = value
            row_parts.append(
                (
                    jnp.sum(value, axis=2, keepdims=True),
                    jnp.sum(value * value, axis=2, keepdims=True),
                )
            )

    contract(0)
    ring_step(1, 2)
    arrive(1, 1)
    contract(-1)
    contract(1)
    scatter(0)
    patch_forwards = []
    for d, copy in zip((1, 3, 2), patch_copies):
        copy.wait_recv()
        piece = m.patch_all.at[2 * lax.rem(x - d + 4, 4) + k]
        patch_forwards.append(
            send(piece, piece, m.patch_send.at[1, d], m.patch_recv.at[1, d], sibling)
        )
    sent += patch_forwards
    ring_step(1, 3)
    arrive(1, 2)
    contract(-2)
    contract(2)
    scatter(1)
    ring_step(1, 4)
    for copy in base_copies:
        copy.wait_recv()
    arrive(1, 3)
    contract(-3)
    contract(3)
    scatter(2)
    collect(0)
    arrive(1, 4)
    contract(4)
    scatter(3)
    for g in range(1, 4):
        collect(g)
    row_sums = sum(part[0] for part in row_parts)
    row_squares = sum(part[1] for part in row_parts)
    row_mean = row_sums * (1.0 / WIDTH)
    row_scale = lax.rsqrt(row_squares * (1.0 / WIDTH) - row_mean * row_mean + EPSILON)
    for copy in (patch_copies[3], *patch_forwards):
        copy.wait_recv()
    projected = jnp.zeros((32, 128), F32)
    for slot in range(8):
        at = lax.rem(z + OFFSETS[slot] + 8, 8)
        value = (m.residual[slot] - row_mean) * row_scale * (1.0 + m.final[2, at]) + m.final[1, at]
        value = value.reshape(16, BLOCK)
        high = value.astype(BF16)
        low = (value - high.astype(F32)).astype(BF16)
        projected += jnp.dot(
            jnp.concatenate([high, low], axis=0), m.patch_all[at], preferred_element_type=F32
        )
    patch = projected[:16, :64] + (projected[16:, :64] + projected[:16, 64:])
    latent = (patch + patch_bias) / 0.3611 + 0.1159
    latent = jnp.concatenate([latent, jnp.zeros((16, 64), F32)], axis=1)
    m.latents[...] = latent
    m.blocks[1, 1, s] = latent

    copies = []
    for ds, dr, dc in halo:
        copy = pltpu.make_async_remote_copy(
            src_ref=m.latents,
            dst_ref=m.blocks.at[1 - dr, 1 - dc, s],
            send_sem=m.halo_send.at[ds, 1 - dr, 1 - dc],
            recv_sem=m.halo_recv.at[ds, 1 - dr, 1 - dc],
            device_id=place(ds, dr, dc),
            device_id_type=MESH,
        )
        copy.start()
        copies.append(copy)

    for copy in copies:
        copy.wait_recv()
    sent += copies

    for ds in range(2):
        for dr in (-1, 0, 1):
            for dc in (-1, 0, 1):
                inside = (r + dr >= 0) & (r + dr < N_ROW) & (c + dc >= 0) & (c + dc < N_COL)
                keep = jnp.where(inside, 1.0, 0.0).astype(jnp.float32)
                block = m.blocks[dr + 1, dc + 1, ds][:, :64] * keep
                rows = {-1: ((1, 0),), 0: ((0, 1), (1, 2)), 1: ((0, 3),)}[dr]
                first, count, at = {-1: (3, 1, 0), 0: (0, 4, 1), 1: (0, 1, 5)}[dc]
                for mb in range(2):
                    for source, target in rows:
                        start = mb * 8 + source * 4 + first
                        m.patches[2 * ds + mb, target, at : at + count, :] = block[
                            start : start + count
                        ]

    slabs = [
        m.patches[:, u : u + 3, v : v + 8, :].reshape(96, 64) for u in range(2) for v in range(2)
    ]
    window = jnp.concatenate(slabs, axis=-1)
    high = window.astype(jnp.bfloat16)
    low = (window - high.astype(jnp.float32)).astype(jnp.bfloat16)
    both = jnp.concatenate([high, low], axis=0)

    jj = lax.broadcasted_iota(jnp.int32, (96, 1), 0) % 8
    ii = (lax.broadcasted_iota(jnp.int32, (96, 1), 0) // 8) % 3
    sums = jnp.zeros((4, 512), jnp.float32)
    squares = jnp.zeros((4, 512), jnp.float32)
    for a in range(2):
        for b in range(2):
            phase = 2 * a + b
            lanes = pl.ds(phase * 512, 512)
            first = jnp.dot(both, m.taps[0, :, lanes], preferred_element_type=jnp.float32)
            second = jnp.dot(high, m.taps[1, :, lanes], preferred_element_type=jnp.float32)
            value = first[:96] + (first[96:] + second) + m.latent_bias[...]
            m.act[phase] = value
            own = (ii >= a) & (ii < a + 2) & (jj >= b) & (jj < b + 4)
            masked = jnp.where(own, value, 0.0).reshape(4, 24, 512)
            sums += jnp.sum(masked, axis=1)
            squares += jnp.sum(masked * masked, axis=1)

    stats = gathered(jnp.concatenate([sums, squares], axis=0), m.member[...])

    m.col_stats[c] = stats
    copies = []
    for dc in range(1, N_COL):
        copy = pltpu.make_async_remote_copy(
            src_ref=m.col_stats.at[c],
            dst_ref=m.col_stats.at[c],
            send_sem=m.col_send.at[dc],
            recv_sem=m.col_recv.at[dc],
            device_id=place(0, 0, dc),
            device_id_type=MESH,
        )
        copy.start()
        copies.append(copy)
    for copy in copies:
        copy.wait_recv()
    sent += copies
    m.row_stats[r] = jnp.sum(m.col_stats[...], axis=0)
    copies = []
    for dr in range(1, N_ROW):
        copy = pltpu.make_async_remote_copy(
            src_ref=m.row_stats.at[r],
            dst_ref=m.row_stats.at[r],
            send_sem=m.row_send.at[dr],
            recv_sem=m.row_recv.at[dr],
            device_id=place(0, dr, 0),
            device_id_type=MESH,
        )
        copy.start()
        copies.append(copy)
    for copy in copies:
        copy.wait_recv()
    sent += copies
    total = jnp.sum(m.row_stats[...], axis=0) * (1.0 / CELLS)
    mean = total[:4]
    scale = lax.rsqrt(total[4:] - mean * mean + EPSILON)
    spread = gathered(jnp.concatenate([mean, scale], axis=0), m.member_t[...])

    for a in range(2):
        for b in range(2):
            phase = 2 * a + b
            line = 4 * r + 2 * ii - a
            across = 8 * c + 2 * jj - b
            inside = (line >= 0) & (line < 64) & (across >= 0) & (across < 64)
            parts = []
            for mb in range(4):
                value = m.act[phase, mb * 24 : mb * 24 + 24]
                value = (value - spread[mb : mb + 1]) * (
                    spread[4 + mb : 5 + mb] * m.gain[...]
                ) + m.shift[...]
                parts.append(value / (1.0 + jnp.exp(-value)))
            value = jnp.where(inside, jnp.concatenate(parts, axis=0), 0.0)
            m.cells[phase * 96 : phase * 96 + 96, :] = value.astype(jnp.bfloat16)

    load_decode.wait()
    for tap in range(9):
        value = jnp.dot(m.cells[...], m.decode_in[tap], preferred_element_type=jnp.float32)
        m.products[tap] = value.reshape(4, 4, 3, 8, 256)

    for a in range(2):
        for b in range(2):
            for up in range(2):
                for left in range(2):
                    total = jnp.zeros((4, 2, 4, 256), jnp.float32) + m.decode_bias[...]
                    for di in range(3):
                        row_phase, row_at = phase_of(a, (up + di - 1) // 2)
                        for dj in range(3):
                            col_phase, col_at = phase_of(b, (left + dj - 1) // 2)
                            total += m.products[
                                di * 3 + dj,
                                row_phase * 2 + col_phase,
                                :,
                                row_at : row_at + 2,
                                col_at : col_at + 4,
                                :,
                            ]
                    for mb in range(4):
                        for i in range(2):
                            for half in range(2):
                                m.staged[
                                    half,
                                    mb,
                                    4 * i + 2 * a + up,
                                    pl.ds(2 * b + left, 4, stride=4),
                                    :,
                                ] = total[mb, i, :, half * 128 : half * 128 + 128]
    stores = [
        load(m.staged.at[half], m.out.at[:, :, :, pl.ds(half * 128, 128)], half)
        for half in range(2)
    ]
    for copy in stores:
        copy.wait()

    for copy in from_partner:
        copy.wait_send()
    for copy in ring.values():
        copy.wait_send()
    for copy in sent:
        copy.wait_send()
    for copy in sib_copies.values():
        copy.wait_send()
    for copy in sum_copies.values():
        copy.wait_send()


def shards(*args):
    shapes = {
        "latent_bias": (1, 512),
        "gain": (1, 512),
        "shift": (1, 512),
        "decode_kernel": (9, 512, 256),
        "decode_bias": (1, 256),
    }
    turned = {"modulation": (1, 0, 2), "reduce": (1, 0), "patch": (1, 0)}
    args = [
        a.transpose(turned[name]) if name in turned else a.reshape(shapes.get(name, a.shape))
        for name, a in zip(INPUTS, args, strict=True)
    ]
    return pl.pallas_call(
        program_kernel,
        out_shape=jax.ShapeDtypeStruct((4, 8, 16, 256), F32),
        in_specs=[pl.BlockSpec(memory_space=space) for space in INPUTS.values()],
        out_specs=pl.BlockSpec(memory_space=pl.ANY),
        scratch_shapes=list(SCRATCH.values()),
        compiler_params=pltpu.CompilerParams(
            collective_id=0, has_side_effects=True, vmem_limit_bytes=58 * 2**20
        ),
    )(*args)


def solution(mesh):
    return jax.shard_map(
        shards,
        mesh=mesh,
        in_specs=(
            P(None, "row", "col"),
            P(),
            P(),
            P("row", "col"),
            P("col"),
            P("col", "row"),
            P("col"),
            P("col", None),
            P(),
            P(),
            P(),
            P(),
            P(),
            P(None, None, None, "section"),
            P("section"),
        ),
        out_specs=P(None, "row", "col", "section"),
        check_vma=False,
    )
```
